32 devices in a mesh: ctx: 8 (over z, y), tp: 4 (over x, core).
Axes of the slice: x: 2, y: 2, z: 4, core: 2. Of those that a mesh axis runs over, the one named last changes fastest.
Arguments:
- queries: bfloat16 [6144, 2048], P('ctx', 'tp'), may hold values from -6 to 6
- keys: bfloat16 [6144, 2048], P('ctx', 'tp'), may hold values from -6 to 6
- values: bfloat16 [6144, 2048], P('ctx', 'tp'), may hold values from -6 to 6
- out_grad: bfloat16 [6144, 2048], P('ctx', 'tp'), may hold values from -6 to 6
- key_blocks: int32 [24, 16], replicated, may hold values from -1 to 23, as said below
- target_counts: int32 [24], replicated, may hold values from 0 to 128, as said below
Outputs:
- query_grad: bfloat16 [6144, 2048], P('ctx', 'tp')
- key_grad: bfloat16 [6144, 2048], P('ctx', 'tp')
- value_grad: bfloat16 [6144, 2048], P('ctx', 'tp')
The draws below stay inside these ranges and needn't reach their ends.
Inputs may be any that keep to these rules, and one draw needn't show every extreme that they name: `key_blocks`: entry 0 of row b is b itself; the other entries are distinct blocks k with b - 6 <= k < b, or -1 for an empty slot; a row has empty slots only where fewer than 15 such blocks exist. The last target_counts[b] events of block b are targets: no other event reads them as keys.
All inputs are finite; a program needn't handle non-finite values.
Results may differ from the reference program's by a relative error of at most 0.005.
Values may be sent and summed in bfloat16 or wider, within the bound.
A program may use at most 64 MiB of HBM per device.

```python
import math
import jax
import jax.numpy as jnp
from jax import lax

HEADS = 16
HEAD = 128
BLK = 256
KPB = 16
BPD = 3
SPAN_TILE_COUNT = 24
TOKENS = 6144
REACH = 2


def draw_key_blocks(key, part):
    key = jax.random.fold_in(key, 11)
    hot_draw, stochastic_ranking_numbers = jax.random.split(key)
    holder_processors = jnp.arange(SPAN_TILE_COUNT, dtype=jnp.int32) // BPD
    frequent_marker_list = jax.random.randint(hot_draw, (SPAN_TILE_COUNT // BPD,), 0, 4) == 0
    frequent_extra_weight = jnp.where(frequent_marker_list[holder_processors], 4096, 0).astype(jnp.int32)
    initial_ranking_number = jax.random.randint(stochastic_ranking_numbers, (SPAN_TILE_COUNT, SPAN_TILE_COUNT), 0, 1024) + frequent_extra_weight[None, :]
    row_index = jnp.arange(SPAN_TILE_COUNT, dtype=jnp.int32)[:, None]
    col_index = jnp.arange(SPAN_TILE_COUNT, dtype=jnp.int32)[None, :]
    eligible_marker = (col_index < row_index) & (col_index >= row_index - REACH * BPD)
    scores = jnp.where(eligible_marker, initial_ranking_number * SPAN_TILE_COUNT + col_index, -1 - col_index)
    top_scores, top_ids = lax.top_k(scores, KPB - 1)
    chosen = jnp.where(top_scores >= 0, top_ids, -1).astype(jnp.int32)
    own_ids = jnp.arange(SPAN_TILE_COUNT, dtype=jnp.int32)[:, None]
    return jnp.concatenate([own_ids, chosen], axis=1).astype(jnp.int32)


def draw_target_counts(key, part):
    key = jax.random.fold_in(key, 7)
    count_draw, place_draw = jax.random.split(key)
    counts = jax.random.randint(count_draw, (SPAN_TILE_COUNT,), 0, BLK // 2 + 1)
    places = jax.random.permutation(place_draw, SPAN_TILE_COUNT)
    counts = counts.at[places[0]].set(BLK // 2)
    counts = counts.at[places[1]].set(0)
    return counts.astype(jnp.int32)


def block_levels(stream_key, shape, cuts, least, top_value):
    gain = 1.0
    for position, parts in cuts:
        steps = jax.random.uniform(jax.random.fold_in(jax.random.fold_in(stream_key, 6), position), (parts,), jnp.float32, least / len(cuts), top_value / len(cuts))
        gain = gain * jnp.repeat(jnp.exp(steps), shape[position] // parts).reshape((-1,) + (1,) * (len(shape) - 1 - position))
    return gain


def gaussian(rng, shape, deviation, most, cuts=(), kind=jnp.bfloat16):
    level = block_levels(rng, shape, cuts, -0.22, 0.18) if cuts else 1.0
    values = jax.random.normal(rng, shape, jnp.float32) * deviation * level
    return jnp.minimum(jnp.maximum(values, -most), most).astype(kind)


def setup_inputs(seed: int = 0) -> dict:
    key_list = jax.random.split(jax.random.key(seed), 7)
    return {
        "queries": gaussian(key_list[0], (TOKENS, HEADS * HEAD), 1.0, 6.0, ((0, 8), (1, 4))),
        "keys": gaussian(key_list[1], (TOKENS, HEADS * HEAD), 1.0, 6.0, ((0, 8), (1, 4))),
        "values": gaussian(key_list[2], (TOKENS, HEADS * HEAD), 1.0, 6.0, ((0, 8), (1, 4))),
        "out_grad": gaussian(key_list[3], (TOKENS, HEADS * HEAD), 1.0, 6.0, ((0, 8), (1, 4))),
        "key_blocks": draw_key_blocks(jax.random.fold_in(key_list[6], 71), 0),
        "target_counts": draw_target_counts(jax.random.fold_in(key_list[6], 71), 0),
    }


def block_mask(query_id, key_id, target_counts):
    row_index = jnp.arange(BLK, dtype=jnp.int32)[:, None]
    col_index = jnp.arange(BLK, dtype=jnp.int32)[None, :]
    own_targets = target_counts[query_id]
    key_targets = target_counts[key_id]
    diagonal = (col_index <= row_index) & ((col_index < BLK - own_targets) | (col_index == row_index))
    earlier = jnp.broadcast_to(col_index < BLK - key_targets, diagonal.shape)
    return jnp.where(query_id == key_id, diagonal, earlier).astype(jnp.float32)

def tile_grads(query_tile, grad_tile, key_tile, value_tile, allowed):
    head_factor = 1.0 / math.sqrt(HEAD)
    norm_scale = 1.0 / math.sqrt(KPB * BLK)
    query_wide = query_tile.astype(jnp.float32)
    grad_wide = grad_tile.astype(jnp.float32)
    key_wide = key_tile.astype(jnp.float32)
    value_wide = value_tile.astype(jnp.float32)
    scores = jnp.einsum('ihd,jhd->hij', query_wide, key_wide) * head_factor
    sigmoid_part = jax.nn.sigmoid(scores)
    gated = allowed[None] * norm_scale
    weights = (scores * sigmoid_part * gated).astype(jnp.bfloat16)
    weight_grad = jnp.einsum('ihd,jhd->hij', grad_wide, value_wide)
    score_grad = (weight_grad * gated * sigmoid_part * (1.0 + scores * (1.0 - sigmoid_part))).astype(jnp.bfloat16)
    score_wide = score_grad.astype(jnp.float32)
    query_part = jnp.einsum('hij,jhd->ihd', score_wide, key_wide) * head_factor
    key_part = jnp.einsum('hij,ihd->jhd', score_wide, query_wide) * head_factor
    payload_portion = jnp.einsum('hij,ihd->jhd', weights.astype(jnp.float32), grad_wide)
    return (query_part, key_part, payload_portion)

def reference(queries, keys, values, out_grad, key_blocks, target_counts):
    block_shape = (SPAN_TILE_COUNT, BLK, HEADS, HEAD)
    query_blocks = queries.reshape(block_shape)
    key_tiles = keys.reshape(block_shape)
    value_tiles = values.reshape(block_shape)
    grad_blocks = out_grad.reshape(block_shape)

    def per_query(state, block_id):
        key_acc, value_acc = state
        query_acc = jnp.zeros((BLK, HEADS, HEAD), jnp.float32)
        for slot in range(KPB):
            listed_id = key_blocks[block_id, slot]
            slot_valid = (listed_id >= 0).astype(jnp.float32)
            safe_id = jnp.maximum(listed_id, 0).astype(jnp.int32)
            allowed = block_mask(block_id, safe_id, target_counts) * slot_valid
            query_part, key_part, payload_portion = tile_grads(query_blocks[block_id], grad_blocks[block_id], key_tiles[safe_id], value_tiles[safe_id], allowed)
            query_acc = query_acc + query_part
            key_acc = key_acc.at[safe_id].add(key_part)
            value_acc = value_acc.at[safe_id].add(payload_portion)
        return ((key_acc, value_acc), query_acc)
    empty = jnp.zeros(block_shape, jnp.float32)
    (key_acc, value_acc), query_acc = lax.scan(per_query, (empty, empty), jnp.arange(SPAN_TILE_COUNT, dtype=jnp.int32))
    flat = (TOKENS, HEADS * HEAD)
    return (query_acc.reshape(flat).astype(jnp.bfloat16), key_acc.reshape(flat).astype(jnp.bfloat16), value_acc.reshape(flat).astype(jnp.bfloat16))
```

```python
import functools
import math

import jax
import jax.numpy as jnp
from jax import lax
from jax.experimental import pallas as pl
from jax.experimental.pallas import tpu as pltpu
from jax.sharding import PartitionSpec as P

HEAD = 128
BLK = 256
KPB = 16
MESH = pl.DeviceIdType.MESH
HEAD_FACTOR = 1.0 / math.sqrt(HEAD)
NORM_SCALE = 1.0 / math.sqrt(KPB * BLK)


def nt(a, b):
    return lax.dot_general(a, b, (((1,), (1,)), ((), ())), preferred_element_type=jnp.float32)


def tn(a, b):
    return lax.dot_general(a, b, (((0,), (0,)), ((), ())), preferred_element_type=jnp.float32)


def tile(query, grad, key, value, allowed=None):
    half = nt(key, query) * (0.5 * HEAD_FACTOR)
    one_tanh = 1.0 + jnp.tanh(half)
    weights = half * one_tanh
    score_grad = nt(value, grad) * (one_tanh * ((1.0 + (half + half)) - weights))
    if allowed is not None:
        weights = jnp.where(allowed, weights, 0.0)
        score_grad = jnp.where(allowed, score_grad, 0.0)
    weights = weights.astype(jnp.bfloat16)
    score_grad = score_grad.astype(jnp.bfloat16)
    value_part = jnp.dot(weights, grad, preferred_element_type=jnp.float32)
    key_part = jnp.dot(score_grad, query, preferred_element_type=jnp.float32)
    query_part = tn(score_grad, key)
    return query_part, key_part, value_part


def kernel(
    n, per, heads,
    blocks_ref, counts_ref, q_ref, g_ref, k_ref, v_ref,
    dq_ref, dk_ref, dv_ref,
    r1q, r1g, r2q, r2g, dq1, dq2, rq1, rq2, dq0, dk_acc, dv_acc, mask,
    z_send, z_recv, y_send, y_recv, d1_send, d1_recv, d2_send, d2_recv,
):
    p = lax.axis_index("ctx")
    total = n * per
    odd = lax.rem(p, 2) == 1
    even = lax.rem(p, 2) == 0
    has1, has2 = p + 1 < n, p + 2 < n
    back1, back2 = p >= 1, p >= 2
    next1, next2 = lax.rem(p + 1, n), lax.rem(p + 2, n)
    prev1, prev2 = lax.rem(p + n - 1, n), lax.rem(p + n - 2, n)
    partner = p + 1 - 2 * lax.rem(p, 2)
    chunks = heads * per
    dq_scale = 0.5 * NORM_SCALE * HEAD_FACTOR

    def part(ref, c):
        rows = pl.ds(pl.multiple_of(lax.rem(c, per) * BLK, BLK), BLK)
        cols = pl.ds(pl.multiple_of(lax.div(c, per) * HEAD, HEAD), HEAD)
        return ref.at[rows, cols]

    def remote(src, dst, c, send, recv, to):
        return pltpu.make_async_remote_copy(
            src_ref=part(src, c), dst_ref=part(dst, c),
            send_sem=send, recv_sem=recv,
            device_id={"ctx": to}, device_id_type=MESH,
        )

    def z_copy(c):
        return [
            remote(src, dst, c, z_send.at[w, c], z_recv.at[w, c], prev2)
            for w, (src, dst) in enumerate(((q_ref, r2q), (g_ref, r2g)))
        ]

    def y_copy(c, sources):
        return [
            remote(src, dst, c, y_send.at[w, c], y_recv.at[w, c], partner)
            for w, (src, dst) in enumerate(zip(sources, (r1q, r1g)))
        ]

    def d1_copy(c):
        return remote(dq1, rq1, c, d1_send.at[c], d1_recv.at[c], next1)

    def d2_copy(c):
        return remote(dq2, rq2, c, d2_send.at[c], d2_recv.at[c], next2)

    barrier = pltpu.get_barrier_semaphore()
    for near, to in ((back1, prev1), (back2, prev2), (has1, next1), (has2, next2)):
        @pl.when(near)
        def _():
            pl.semaphore_signal(barrier, inc=1, device_id={"ctx": to}, device_id_type=MESH)
    pl.semaphore_wait(barrier, jnp.minimum(p, 2) + jnp.minimum(n - 1 - p, 2))

    def first_sends(c, carry):
        @pl.when(back2)
        def _():
            for copy in z_copy(c):
                copy.start()

        @pl.when(odd)
        def _():
            for copy in y_copy(c, (q_ref, g_ref)):
                copy.start()
        return carry

    lax.fori_loop(0, chunks, first_sends, 0)

    row = lax.broadcasted_iota(jnp.int32, (BLK, HEAD), 0)
    for j in range(per):
        key_id = p * per + j
        kept = row < BLK - counts_ref[key_id]
        for d in range(3):
            for i in range(per):
                if (d == 0 and j >= i) or (d == 2 and j < i):
                    continue
                query_id = jnp.minimum((p + d) * per + i, total - 1)
                listed = jnp.int32(0)
                for slot in range(1, KPB):
                    listed = jnp.where(blocks_ref[query_id, slot] == key_id, 1, listed)
                mask[d * per + i, pl.ds(j * BLK, BLK), :] = jnp.where(
                    kept, listed.astype(jnp.float32), 0.0
                ).astype(jnp.bfloat16)

    key_row = lax.broadcasted_iota(jnp.int32, (BLK, BLK), 0)
    query_col = lax.broadcasted_iota(jnp.int32, (BLK, BLK), 1)

    def per_head(h, carry):
        cols = pl.ds(pl.multiple_of(h * HEAD, HEAD), HEAD)
        dk_acc[...] = jnp.zeros_like(dk_acc)
        dv_acc[...] = jnp.zeros_like(dv_acc)

        def source(d, i, query_ref, grad_ref):
            rows = pl.ds(i * BLK, BLK)
            query, grad = query_ref[rows, cols], grad_ref[rows, cols]
            query_sum = None
            key_slots = {0: range(0, i + 1), 1: range(per), 2: range(i, per)}[d]
            for j in key_slots:
                at = pl.ds(j * BLK, BLK)
                key, value, allowed = k_ref[at, cols], v_ref[at, cols], None
                if d == 0 and j == i:
                    limit = BLK - counts_ref[p * per + i]
                    allowed = (key_row <= query_col) & (
                        (key_row < limit) | (key_row == query_col)
                    )
                else:
                    read = mask[d * per + i, at, :]
                    key, value = key * read, value * read
                query_part, key_part, value_part = tile(query, grad, key, value, allowed)
                query_sum = query_part if query_sum is None else query_sum + query_part
                dk_acc[at, :] += key_part
                dv_acc[at, :] += value_part
            return query_sum * dq_scale

        for i in range(per):
            c = h * per + i
            rows = pl.ds(i * BLK, BLK)

            @pl.when(has2)
            def _():
                for copy in z_copy(c):
                    copy.wait_recv()

                @pl.when(even)
                def _():
                    for copy in y_copy(c, (r2q, r2g)):
                        copy.start()

            dq0[rows, cols] = source(0, i, q_ref, g_ref)

            @pl.when(has2)
            def _():
                dq2[rows, cols] = source(2, i, r2q, r2g).astype(jnp.bfloat16)
                d2_copy(c).start()

            @pl.when(has1)
            def _():
                for copy in y_copy(c, (q_ref, g_ref)):
                    copy.wait_recv()
                dq1[rows, cols] = source(1, i, r1q, r1g).astype(jnp.bfloat16)
                d1_copy(c).start()

        dk_ref[:, cols] = (dk_acc[...] * dq_scale).astype(jnp.bfloat16)
        dv_ref[:, cols] = (dv_acc[...] * NORM_SCALE).astype(jnp.bfloat16)
        return carry

    lax.fori_loop(0, heads, per_head, 0)

    def finish(c, carry):
        rows = pl.ds(pl.multiple_of(lax.rem(c, per) * BLK, BLK), BLK)
        cols = pl.ds(pl.multiple_of(lax.div(c, per) * HEAD, HEAD), HEAD)

        @pl.when(back2)
        def _():
            d2_copy(c).wait_recv()
            dq0[rows, cols] += rq2[rows, cols].astype(jnp.float32)
            for copy in z_copy(c):
                copy.wait_send()

        @pl.when(back1)
        def _():
            d1_copy(c).wait_recv()
            dq0[rows, cols] += rq1[rows, cols].astype(jnp.float32)

        dq_ref[rows, cols] = dq0[rows, cols].astype(jnp.bfloat16)

        @pl.when(odd | has2)
        def _():
            for copy in y_copy(c, (q_ref, g_ref)):
                copy.wait_send()

        @pl.when(has1)
        def _():
            d1_copy(c).wait_send()

        @pl.when(has2)
        def _():
            d2_copy(c).wait_send()
        return carry

    lax.fori_loop(0, chunks, finish, 0)


def near_body(n, queries, keys, values, out_grad, key_blocks, target_counts):
    rows, columns = queries.shape
    per, heads = rows // BLK, columns // HEAD
    chunks = heads * per
    narrow = pltpu.VMEM((rows, columns), jnp.bfloat16)
    wide = pltpu.VMEM((rows, columns), jnp.float32)
    acc = pltpu.VMEM((rows, HEAD), jnp.float32)
    pair = pltpu.SemaphoreType.DMA((2, chunks))
    single = pltpu.SemaphoreType.DMA((chunks,))
    whole = pl.BlockSpec(memory_space=pltpu.VMEM)
    scalars = pl.BlockSpec(memory_space=pltpu.SMEM)
    result = jax.ShapeDtypeStruct((rows, columns), jnp.bfloat16)
    return pl.pallas_call(
        functools.partial(kernel, n, per, heads),
        out_shape=(result, result, result),
        in_specs=[scalars, scalars] + [whole] * 4,
        out_specs=(whole, whole, whole),
        scratch_shapes=[narrow] * 8
        + [wide, acc, acc, pltpu.VMEM((3 * per, rows, HEAD), jnp.bfloat16)]
        + [pair] * 4 + [single] * 4,
        compiler_params=pltpu.CompilerParams(
            collective_id=0, has_side_effects=True, vmem_limit_bytes=48 * 1024 * 1024
        ),
    )(key_blocks, target_counts, queries, out_grad, keys, values)


def from_behind(array, axis, by):
    length = lax.axis_size(axis)
    pairs = [(i, i + by) for i in range(length) if 0 <= i + by < length]
    return lax.ppermute(array, axis, pairs)


def passed_along(array, axis, by):
    length = lax.axis_size(axis)
    return lax.ppermute(array, axis, [(i, (i + by) % length) for i in range(length)])


def block_mask(query_id, key_id, target_counts):
    row_index = jnp.arange(BLK, dtype=jnp.int32)[:, None]
    col_index = jnp.arange(BLK, dtype=jnp.int32)[None, :]
    own_targets = target_counts[query_id]
    key_targets = target_counts[key_id]
    diagonal = (col_index <= row_index) & (
        (col_index < BLK - own_targets) | (col_index == row_index)
    )
    earlier = jnp.broadcast_to(col_index < BLK - key_targets, diagonal.shape)
    return jnp.where(query_id == key_id, diagonal, earlier).astype(jnp.float32)


def tile_grads(query_tile, grad_tile, key_tile, value_tile, allowed):
    head_factor = 1.0 / math.sqrt(HEAD)
    norm_scale = 1.0 / math.sqrt(KPB * BLK)
    scores = (
        jnp.einsum("ihd,jhd->hij", query_tile, key_tile, preferred_element_type=jnp.float32)
        * head_factor
    )
    sigmoid_part = jax.nn.sigmoid(scores)
    gated = allowed[None] * norm_scale
    weights = (scores * sigmoid_part * gated).astype(jnp.bfloat16)
    weight_grad = jnp.einsum(
        "ihd,jhd->hij", grad_tile, value_tile, preferred_element_type=jnp.float32
    )
    score_grad = (
        weight_grad * gated * sigmoid_part * (1.0 + scores * (1.0 - sigmoid_part))
    ).astype(jnp.bfloat16)
    query_part = (
        jnp.einsum("hij,jhd->ihd", score_grad, key_tile, preferred_element_type=jnp.float32)
        * head_factor
    )
    key_part = (
        jnp.einsum("hij,ihd->jhd", score_grad, query_tile, preferred_element_type=jnp.float32)
        * head_factor
    )
    payload_portion = jnp.einsum(
        "hij,ihd->jhd", weights, grad_tile, preferred_element_type=jnp.float32
    )
    return (query_part, key_part, payload_portion)


def visit(
    query_base,
    key_base,
    active,
    query_here,
    grad_here,
    key_here,
    value_here,
    grads,
    key_blocks,
    target_counts,
):
    per_device = query_here.shape[0]
    total_blocks = key_blocks.shape[0]

    def pair_step(pair_index, present_value):
        query_slot = pair_index // per_device
        key_slot = pair_index % per_device
        query_id = jnp.clip(query_base + query_slot, 0, total_blocks - 1)
        key_id = key_base + key_slot
        listed = active & jnp.any(key_blocks[query_id] == key_id)

        def work(accums):
            query_acc, key_acc, value_acc = accums
            safe_key = jnp.clip(key_id, 0, total_blocks - 1)
            allowed = block_mask(query_id, safe_key, target_counts)
            query_part, key_part, payload_portion = tile_grads(
                query_here[query_slot],
                grad_here[query_slot],
                key_here[key_slot],
                value_here[key_slot],
                allowed,
            )
            return (
                query_acc.at[query_slot].add(query_part),
                key_acc.at[key_slot].add(key_part),
                value_acc.at[key_slot].add(payload_portion),
            )

        return lax.cond(listed, work, lambda unchanged: unchanged, present_value)

    return lax.fori_loop(0, per_device * per_device, pair_step, grads)


def body(queries, keys, values, out_grad, key_blocks, target_counts):
    cycle_size = lax.axis_size("ctx")
    reach_hops = cycle_size // 4
    position = lax.axis_index("ctx")
    per_device = queries.shape[0] // BLK
    heads_here = queries.shape[1] // HEAD
    block_shape = (per_device, BLK, heads_here, HEAD)
    query_blocks = queries.reshape(block_shape)
    key_tiles = keys.reshape(block_shape)
    value_tiles = values.reshape(block_shape)
    grad_blocks = out_grad.reshape(block_shape)
    empty = jnp.zeros(block_shape, jnp.float32)

    def query_hop(hop_index, state):
        query_here, grad_here, query_acc, key_acc, value_acc = state
        source = position + hop_index
        query_acc, key_acc, value_acc = visit(
            source * per_device,
            position * per_device,
            source < cycle_size,
            query_here,
            grad_here,
            key_tiles,
            value_tiles,
            (query_acc, key_acc, value_acc),
            key_blocks,
            target_counts,
        )
        query_here, grad_here = from_behind((query_here, grad_here), "ctx", -1)
        query_acc = passed_along(query_acc, "ctx", -1)
        return (query_here, grad_here, query_acc, key_acc, value_acc)

    state = lax.fori_loop(
        0, reach_hops, query_hop, (query_blocks, grad_blocks, empty, empty, empty)
    )
    query_here, grad_here, query_acc, key_acc, value_acc = state
    source = position + reach_hops
    query_acc, key_acc, value_acc = visit(
        source * per_device,
        position * per_device,
        source < cycle_size,
        query_here,
        grad_here,
        key_tiles,
        value_tiles,
        (query_acc, key_acc, value_acc),
        key_blocks,
        target_counts,
    )
    query_acc = passed_along(query_acc.astype(jnp.bfloat16), "ctx", reach_hops).astype(
        query_acc.dtype
    )
    flat = queries.shape
    return (
        query_acc.reshape(flat).astype(jnp.bfloat16),
        key_acc.reshape(flat).astype(jnp.bfloat16),
        value_acc.reshape(flat).astype(jnp.bfloat16),
    )


def solution(mesh):
    in_specs = (P("ctx", "tp"), P("ctx", "tp"), P("ctx", "tp"), P("ctx", "tp"), P(), P())
    out_specs = (P("ctx", "tp"), P("ctx", "tp"), P("ctx", "tp"))
    length = mesh.shape["ctx"]
    mapped = functools.partial(near_body, length) if length // 4 == 2 else body
    return jax.shard_map(
        mapped, mesh=mesh, in_specs=in_specs, out_specs=out_specs, check_vma=False
    )
```

```python
import functools
import math

import jax
import jax.numpy as jnp
from jax import lax
from jax.experimental import pallas as pl
from jax.experimental.pallas import tpu as pltpu
from jax.sharding import PartitionSpec as P

HEAD = 128
BLK = 256
KPB = 16
MESH = pl.DeviceIdType.MESH
HEAD_FACTOR = 1.0 / math.sqrt(HEAD)
NORM_SCALE = 1.0 / math.sqrt(KPB * BLK)


def nt(a, b):
    return lax.dot_general(a, b, (((1,), (1,)), ((), ())), preferred_element_type=jnp.float32)


def tn(a, b):
    return lax.dot_general(a, b, (((0,), (0,)), ((), ())), preferred_element_type=jnp.float32)


def tile(query, grad, key, value, allowed=None):
    half = nt(key, query) * (0.5 * HEAD_FACTOR)
    one_tanh = 1.0 + jnp.tanh(half)
    weights = half * one_tanh
    score_grad = nt(value, grad) * (one_tanh * ((1.0 + (half + half)) - weights))
    if allowed is not None:
        weights = jnp.where(allowed, weights, 0.0)
        score_grad = jnp.where(allowed, score_grad, 0.0)
    weights = weights.astype(jnp.bfloat16)
    score_grad = score_grad.astype(jnp.bfloat16)
    value_part = jnp.dot(weights, grad, preferred_element_type=jnp.float32)
    key_part = jnp.dot(score_grad, query, preferred_element_type=jnp.float32)
    query_part = tn(score_grad, key)
    return query_part, key_part, value_part


def kernel(
    n, per, heads,
    blocks_ref, counts_ref, q_hbm, g_hbm, k_hbm, v_hbm,
    dq_hbm, dk_hbm, dv_hbm,
    dq_ref, dk_ref, dv_ref, q_ref, g_ref, k_ref, v_ref, r1q, r1g, r2q, r2g, dq1, dq2, rq1, rq2, dq0, dk_acc, dv_acc, mask,
    z_send, z_recv, y_send, y_recv, d1_send, d1_recv, d2_send, d2_recv, own, dq_out, dkv_out,
):
    p = lax.axis_index("ctx")
    total = n * per
    odd = lax.rem(p, 2) == 1
    even = lax.rem(p, 2) == 0
    has1, has2 = p + 1 < n, p + 2 < n
    back1, back2 = p >= 1, p >= 2
    next1, next2 = lax.rem(p + 1, n), lax.rem(p + 2, n)
    prev1, prev2 = lax.rem(p + n - 1, n), lax.rem(p + n - 2, n)
    partner = p + 1 - 2 * lax.rem(p, 2)
    chunks = heads * per
    dq_scale = 0.5 * NORM_SCALE * HEAD_FACTOR

    def part(ref, c):
        rows = pl.ds(pl.multiple_of(lax.rem(c, per) * BLK, BLK), BLK)
        cols = pl.ds(pl.multiple_of(lax.div(c, per) * HEAD, HEAD), HEAD)
        return ref.at[rows, cols]

    def remote(src, dst, c, send, recv, to):
        return pltpu.make_async_remote_copy(
            src_ref=part(src, c), dst_ref=part(dst, c),
            send_sem=send, recv_sem=recv,
            device_id={"ctx": to}, device_id_type=MESH,
        )

    def dq_store(c):
        return pltpu.make_async_copy(part(dq_ref, c), part(dq_hbm, c), dq_out.at[c])

    def dkv_store(h):
        cols = pl.ds(pl.multiple_of(h * HEAD, HEAD), HEAD)
        return [
            pltpu.make_async_copy(src.at[:, cols], dst.at[:, cols], dkv_out.at[w, h])
            for w, (src, dst) in enumerate(((dk_ref, dk_hbm), (dv_ref, dv_hbm)))
        ]

    def z_copy(c):
        return [
            remote(src, dst, c, z_send.at[w, c], z_recv.at[w, c], prev2)
            for w, (src, dst) in enumerate(((q_hbm, r2q), (g_hbm, r2g)))
        ]

    def y_copy(c, sources):
        return [
            remote(src, dst, c, y_send.at[w, c], y_recv.at[w, c], partner)
            for w, (src, dst) in enumerate(zip(sources, (r1q, r1g)))
        ]

    def d1_copy(c):
        return remote(dq1, rq1, c, d1_send.at[c], d1_recv.at[c], next1)

    def d2_copy(c):
        return remote(dq2, rq2, c, d2_send.at[c], d2_recv.at[c], next2)

    loads = [
        pltpu.make_async_copy(src, dst, own.at[w])
        for w, (src, dst) in enumerate(
            ((k_hbm, k_ref), (v_hbm, v_ref), (q_hbm, q_ref), (g_hbm, g_ref))
        )
    ]

    barrier = pltpu.get_barrier_semaphore()
    for near, to in ((back1, prev1), (back2, prev2), (has1, next1), (has2, next2)):
        @pl.when(near)
        def _():
            pl.semaphore_signal(barrier, inc=1, device_id={"ctx": to}, device_id_type=MESH)
    pl.semaphore_wait(barrier, jnp.minimum(p, 2) + jnp.minimum(n - 1 - p, 2))

    def first_sends(c, carry):
        @pl.when(back2)
        def _():
            for copy in z_copy(c):
                copy.start()

        @pl.when(odd)
        def _():
            for copy in y_copy(c, (q_hbm, g_hbm)):
                copy.start()
        return carry

    lax.fori_loop(0, chunks, first_sends, 0)
    for load in loads:
        load.start()

    row = lax.broadcasted_iota(jnp.int32, (BLK, HEAD), 0)
    for j in range(per):
        key_id = p * per + j
        kept = row < BLK - counts_ref[key_id]
        for d in range(3):
            for i in range(per):
                if (d == 0 and j >= i) or (d == 2 and j < i):
                    continue
                query_id = jnp.minimum((p + d) * per + i, total - 1)
                listed = jnp.int32(0)
                for slot in range(1, KPB):
                    listed = jnp.where(blocks_ref[slot, query_id] == key_id, 1, listed)
                mask[d * per + i, pl.ds(j * BLK, BLK), :] = jnp.where(
                    kept, listed.astype(jnp.float32), 0.0
                ).astype(jnp.bfloat16)

    key_row = lax.broadcasted_iota(jnp.int32, (BLK, BLK), 0)
    query_col = lax.broadcasted_iota(jnp.int32, (BLK, BLK), 1)

    for load in loads:
        load.wait()
    late = even & has2

    def per_head(h, carry):
        cols = pl.ds(pl.multiple_of(h * HEAD, HEAD), HEAD)
        dk_acc[...] = jnp.zeros_like(dk_acc)
        dv_acc[...] = jnp.zeros_like(dv_acc)

        def source(d, i, query_ref, grad_ref):
            rows = pl.ds(i * BLK, BLK)
            query, grad = query_ref[rows, cols], grad_ref[rows, cols]
            query_sum = None
            key_slots = {0: range(0, i + 1), 1: range(per), 2: range(i, per)}[d]
            for j in key_slots:
                at = pl.ds(j * BLK, BLK)
                key, value, allowed = k_ref[at, cols], v_ref[at, cols], None
                if d == 0 and j == i:
                    limit = BLK - counts_ref[p * per + i]
                    allowed = (key_row <= query_col) & (
                        (key_row < limit) | (key_row == query_col)
                    )
                else:
                    read = mask[d * per + i, at, :]
                    key, value = key * read, value * read
                query_part, key_part, value_part = tile(query, grad, key, value, allowed)
                query_sum = query_part if query_sum is None else query_sum + query_part
                dk_acc[at, :] += key_part
                dv_acc[at, :] += value_part
            return query_sum * dq_scale

        for i in range(per):
            c = h * per + i
            rows = pl.ds(i * BLK, BLK)

            @pl.when(has2)
            def _():
                for copy in z_copy(c):
                    copy.wait_recv()

                @pl.when(even)
                def _():
                    for copy in y_copy(c, (r2q, r2g)):
                        copy.start()

            dq0[rows, cols] = source(0, i, q_ref, g_ref)

            @pl.when(has2)
            def _():
                dq2[rows, cols] = source(2, i, r2q, r2g).astype(jnp.bfloat16)
                d2_copy(c).start()

            @pl.when(has1)
            def _():
                for copy in y_copy(c, (q_hbm, g_hbm)):
                    copy.wait_recv()
                dq1[rows, cols] = source(1, i, r1q, r1g).astype(jnp.bfloat16)

                @pl.when(jnp.logical_not(late))
                def _():
                    d1_copy(c).start()

        dk_ref[:, cols] = (dk_acc[...] * dq_scale).astype(jnp.bfloat16)
        dv_ref[:, cols] = (dv_acc[...] * NORM_SCALE).astype(jnp.bfloat16)
        for store in dkv_store(h):
            store.start()
        return carry

    lax.fori_loop(0, heads, per_head, 0)

    def late_sends(c, carry):
        d1_copy(c).start()
        return carry

    @pl.when(late)
    def _():
        lax.fori_loop(0, chunks, late_sends, 0)

    def finish(c, carry):
        rows = pl.ds(pl.multiple_of(lax.rem(c, per) * BLK, BLK), BLK)
        cols = pl.ds(pl.multiple_of(lax.div(c, per) * HEAD, HEAD), HEAD)

        @pl.when(back2)
        def _():
            d2_copy(c).wait_recv()
            dq0[rows, cols] += rq2[rows, cols].astype(jnp.float32)
            for copy in z_copy(c):
                copy.wait_send()

        @pl.when(back1)
        def _():
            d1_copy(c).wait_recv()
            dq0[rows, cols] += rq1[rows, cols].astype(jnp.float32)

        dq_ref[rows, cols] = dq0[rows, cols].astype(jnp.bfloat16)
        dq_store(c).start()

        @pl.when(odd | has2)
        def _():
            for copy in y_copy(c, (q_hbm, g_hbm)):
                copy.wait_send()

        @pl.when(has1)
        def _():
            d1_copy(c).wait_send()

        @pl.when(has2)
        def _():
            d2_copy(c).wait_send()
        return carry

    lax.fori_loop(0, chunks, finish, 0)

    def stored(h, carry):
        for store in dkv_store(h):
            store.wait()
        for i in range(per):
            dq_store(h * per + i).wait()
        return carry

    lax.fori_loop(0, heads, stored, 0)


def hand_over(a_in, b_in, c_in, a_out, b_out, c_out, done):
    copies = [
        pltpu.make_async_copy(src, dst, done.at[w])
        for w, (src, dst) in enumerate(((a_in, a_out), (b_in, b_out), (c_in, c_out)))
    ]
    for copy in copies:
        copy.start()
    for copy in copies:
        copy.wait()


def near_body(n, queries, keys, values, out_grad, key_blocks, target_counts):
    rows, columns = queries.shape
    per, heads = rows // BLK, columns // HEAD
    chunks = heads * per
    narrow = pltpu.VMEM((rows, columns), jnp.bfloat16)
    wide = pltpu.VMEM((rows, columns), jnp.float32)
    acc = pltpu.VMEM((rows, HEAD), jnp.float32)
    pair = pltpu.SemaphoreType.DMA((2, chunks))
    single = pltpu.SemaphoreType.DMA((chunks,))
    scalars = pl.BlockSpec(memory_space=pltpu.SMEM)
    result = jax.ShapeDtypeStruct((rows, columns), jnp.bfloat16)
    grads = pl.pallas_call(
        functools.partial(kernel, n, per, heads),
        out_shape=(result, result, result),
        in_specs=[scalars, scalars] + [pl.BlockSpec(memory_space=pl.ANY)] * 4,
        out_specs=(pl.BlockSpec(memory_space=pl.ANY),) * 3,
        scratch_shapes=[narrow] * 15
        + [wide, acc, acc, pltpu.VMEM((3 * per, rows, HEAD), jnp.bfloat16)]
        + [pair] * 4 + [single] * 4 + [pltpu.SemaphoreType.DMA((4,)), single, pltpu.SemaphoreType.DMA((2, heads))],
        compiler_params=pltpu.CompilerParams(
            collective_id=0, has_side_effects=True, vmem_limit_bytes=56 * 1024 * 1024
        ),
    )(key_blocks.T, target_counts, queries, out_grad, keys, values)
    return pl.pallas_call(
        hand_over,
        out_shape=(result, result, result),
        in_specs=[pl.BlockSpec(memory_space=pl.ANY)] * 3,
        out_specs=(pl.BlockSpec(memory_space=pl.ANY),) * 3,
        scratch_shapes=[pltpu.SemaphoreType.DMA((3,))],
        compiler_params=pltpu.CompilerParams(vmem_limit_bytes=56 * 1024 * 1024),
    )(*grads)


def from_behind(array, axis, by):
    length = lax.axis_size(axis)
    pairs = [(i, i + by) for i in range(length) if 0 <= i + by < length]
    return lax.ppermute(array, axis, pairs)


def passed_along(array, axis, by):
    length = lax.axis_size(axis)
    return lax.ppermute(array, axis, [(i, (i + by) % length) for i in range(length)])


def block_mask(query_id, key_id, target_counts):
    row_index = jnp.arange(BLK, dtype=jnp.int32)[:, None]
    col_index = jnp.arange(BLK, dtype=jnp.int32)[None, :]
    own_targets = target_counts[query_id]
    key_targets = target_counts[key_id]
    diagonal = (col_index <= row_index) & (
        (col_index < BLK - own_targets) | (col_index == row_index)
    )
    earlier = jnp.broadcast_to(col_index < BLK - key_targets, diagonal.shape)
    return jnp.where(query_id == key_id, diagonal, earlier).astype(jnp.float32)


def tile_grads(query_tile, grad_tile, key_tile, value_tile, allowed):
    head_factor = 1.0 / math.sqrt(HEAD)
    norm_scale = 1.0 / math.sqrt(KPB * BLK)
    scores = (
        jnp.einsum("ihd,jhd->hij", query_tile, key_tile, preferred_element_type=jnp.float32)
        * head_factor
    )
    sigmoid_part = jax.nn.sigmoid(scores)
    gated = allowed[None] * norm_scale
    weights = (scores * sigmoid_part * gated).astype(jnp.bfloat16)
    weight_grad = jnp.einsum(
        "ihd,jhd->hij", grad_tile, value_tile, preferred_element_type=jnp.float32
    )
    score_grad = (
        weight_grad * gated * sigmoid_part * (1.0 + scores * (1.0 - sigmoid_part))
    ).astype(jnp.bfloat16)
    query_part = (
        jnp.einsum("hij,jhd->ihd", score_grad, key_tile, preferred_element_type=jnp.float32)
        * head_factor
    )
    key_part = (
        jnp.einsum("hij,ihd->jhd", score_grad, query_tile, preferred_element_type=jnp.float32)
        * head_factor
    )
    payload_portion = jnp.einsum(
        "hij,ihd->jhd", weights, grad_tile, preferred_element_type=jnp.float32
    )
    return (query_part, key_part, payload_portion)


def visit(
    query_base,
    key_base,
    active,
    query_here,
    grad_here,
    key_here,
    value_here,
    grads,
    key_blocks,
    target_counts,
):
    per_device = query_here.shape[0]
    total_blocks = key_blocks.shape[0]

    def pair_step(pair_index, present_value):
        query_slot = pair_index // per_device
        key_slot = pair_index % per_device
        query_id = jnp.clip(query_base + query_slot, 0, total_blocks - 1)
        key_id = key_base + key_slot
        listed = active & jnp.any(key_blocks[query_id] == key_id)

        def work(accums):
            query_acc, key_acc, value_acc = accums
            safe_key = jnp.clip(key_id, 0, total_blocks - 1)
            allowed = block_mask(query_id, safe_key, target_counts)
            query_part, key_part, payload_portion = tile_grads(
                query_here[query_slot],
                grad_here[query_slot],
                key_here[key_slot],
                value_here[key_slot],
                allowed,
            )
            return (
                query_acc.at[query_slot].add(query_part),
                key_acc.at[key_slot].add(key_part),
                value_acc.at[key_slot].add(payload_portion),
            )

        return lax.cond(listed, work, lambda unchanged: unchanged, present_value)

    return lax.fori_loop(0, per_device * per_device, pair_step, grads)


def body(queries, keys, values, out_grad, key_blocks, target_counts):
    cycle_size = lax.axis_size("ctx")
    reach_hops = cycle_size // 4
    position = lax.axis_index("ctx")
    per_device = queries.shape[0] // BLK
    heads_here = queries.shape[1] // HEAD
    block_shape = (per_device, BLK, heads_here, HEAD)
    query_blocks = queries.reshape(block_shape)
    key_tiles = keys.reshape(block_shape)
    value_tiles = values.reshape(block_shape)
    grad_blocks = out_grad.reshape(block_shape)
    empty = jnp.zeros(block_shape, jnp.float32)

    def query_hop(hop_index, state):
        query_here, grad_here, query_acc, key_acc, value_acc = state
        source = position + hop_index
        query_acc, key_acc, value_acc = visit(
            source * per_device,
            position * per_device,
            source < cycle_size,
            query_here,
            grad_here,
            key_tiles,
            value_tiles,
            (query_acc, key_acc, value_acc),
            key_blocks,
            target_counts,
        )
        query_here, grad_here = from_behind((query_here, grad_here), "ctx", -1)
        query_acc = passed_along(query_acc, "ctx", -1)
        return (query_here, grad_here, query_acc, key_acc, value_acc)

    state = lax.fori_loop(
        0, reach_hops, query_hop, (query_blocks, grad_blocks, empty, empty, empty)
    )
    query_here, grad_here, query_acc, key_acc, value_acc = state
    source = position + reach_hops
    query_acc, key_acc, value_acc = visit(
        source * per_device,
        position * per_device,
        source < cycle_size,
        query_here,
        grad_here,
        key_tiles,
        value_tiles,
        (query_acc, key_acc, value_acc),
        key_blocks,
        target_counts,
    )
    query_acc = passed_along(query_acc.astype(jnp.bfloat16), "ctx", reach_hops).astype(
        query_acc.dtype
    )
    flat = queries.shape
    return (
        query_acc.reshape(flat).astype(jnp.bfloat16),
        key_acc.reshape(flat).astype(jnp.bfloat16),
        value_acc.reshape(flat).astype(jnp.bfloat16),
    )


def solution(mesh):
    in_specs = (P("ctx", "tp"), P("ctx", "tp"), P("ctx", "tp"), P("ctx", "tp"), P(), P())
    out_specs = (P("ctx", "tp"), P("ctx", "tp"), P("ctx", "tp"))
    length = mesh.shape["ctx"]
    mapped = functools.partial(near_body, length) if length // 4 == 2 else body
    return jax.shard_map(
        mapped, mesh=mesh, in_specs=in_specs, out_specs=out_specs, check_vma=False
    )
```

```python
import functools
import math

import jax
import jax.numpy as jnp
from jax import lax
from jax.experimental import pallas as pl
from jax.experimental.pallas import tpu as pltpu
from jax.sharding import PartitionSpec as P

HEAD = 128
BLK = 256
KPB = 16
MESH = pl.DeviceIdType.MESH
HEAD_FACTOR = 1.0 / math.sqrt(HEAD)
NORM_SCALE = 1.0 / math.sqrt(KPB * BLK)


def nt(a, b):
    return lax.dot_general(a, b, (((1,), (1,)), ((), ())), preferred_element_type=jnp.float32)


def tn(a, b):
    return lax.dot_general(a, b, (((0,), (0,)), ((), ())), preferred_element_type=jnp.float32)


def tile(query, grad, key, value, allowed=None):
    half = nt(key, query) * (0.5 * HEAD_FACTOR)
    one_tanh = 1.0 + jnp.tanh(half)
    weights = half * one_tanh
    score_grad = nt(value, grad) * (one_tanh * ((1.0 + (half + half)) - weights))
    if allowed is not None:
        weights = jnp.where(allowed, weights, 0.0)
        score_grad = jnp.where(allowed, score_grad, 0.0)
    weights = weights.astype(jnp.bfloat16)
    score_grad = score_grad.astype(jnp.bfloat16)
    value_part = jnp.dot(weights, grad, preferred_element_type=jnp.float32)
    key_part = jnp.dot(score_grad, query, preferred_element_type=jnp.float32)
    query_part = tn(score_grad, key)
    return query_part, key_part, value_part


def kernel(
    n, per, heads,
    blocks_ref, counts_ref, q_hbm, g_hbm, k_hbm, v_hbm,
    dq_hbm, dk_hbm, dv_hbm,
    dq_ref, dk_ref, dv_ref, q_ref, g_ref, k_ref, v_ref, r1q, r1g, r2q, r2g, dq1, dq2, rq1, rq2, dq0, dk_acc, dv_acc, mask,
    z_send, z_recv, y_send, y_recv, d1_send, d1_recv, d2_send, d2_recv, own, dq_out, dkv_out,
):
    p = lax.axis_index("ctx")
    total = n * per
    odd = lax.rem(p, 2) == 1
    even = lax.rem(p, 2) == 0
    has1, has2 = p + 1 < n, p + 2 < n
    back1, back2 = p >= 1, p >= 2
    next1, next2 = lax.rem(p + 1, n), lax.rem(p + 2, n)
    prev1, prev2 = lax.rem(p + n - 1, n), lax.rem(p + n - 2, n)
    partner = p + 1 - 2 * lax.rem(p, 2)
    chunks = heads * per
    dq_scale = 0.5 * NORM_SCALE * HEAD_FACTOR

    def part(ref, c):
        rows = pl.ds(pl.multiple_of(lax.rem(c, per) * BLK, BLK), BLK)
        cols = pl.ds(pl.multiple_of(lax.div(c, per) * HEAD, HEAD), HEAD)
        return ref.at[rows, cols]

    def remote(src, dst, c, send, recv, to):
        return pltpu.make_async_remote_copy(
            src_ref=part(src, c), dst_ref=part(dst, c),
            send_sem=send, recv_sem=recv,
            device_id={"ctx": to}, device_id_type=MESH,
        )

    def dq_store(c):
        return pltpu.make_async_copy(part(dq_ref, c), part(dq_hbm, c), dq_out.at[c])

    def dkv_store(h):
        cols = pl.ds(pl.multiple_of(h * HEAD, HEAD), HEAD)
        return [
            pltpu.make_async_copy(src.at[:, cols], dst.at[:, cols], dkv_out.at[w, h])
            for w, (src, dst) in enumerate(((dk_ref, dk_hbm), (dv_ref, dv_hbm)))
        ]

    def z_copy(c):
        return [
            remote(src, dst, c, z_send.at[w, c], z_recv.at[w, c], prev2)
            for w, (src, dst) in enumerate(((q_ref, r2q), (g_ref, r2g)))
        ]

    def y_copy(c, sources):
        return [
            remote(src, dst, c, y_send.at[w, c], y_recv.at[w, c], partner)
            for w, (src, dst) in enumerate(zip(sources, (r1q, r1g)))
        ]

    def d1_copy(c):
        return remote(dq1, rq1, c, d1_send.at[c], d1_recv.at[c], next1)

    def d2_copy(c):
        return remote(dq2, rq2, c, d2_send.at[c], d2_recv.at[c], next2)

    loads = [
        pltpu.make_async_copy(src, dst, own.at[w])
        for w, (src, dst) in enumerate(
            ((q_hbm, q_ref), (g_hbm, g_ref), (k_hbm, k_ref), (v_hbm, v_ref))
        )
    ]

    for load in loads:
        load.start()

    barrier = pltpu.get_barrier_semaphore()
    for near, to in ((back1, prev1), (back2, prev2), (has1, next1), (has2, next2)):
        @pl.when(near)
        def _():
            pl.semaphore_signal(barrier, inc=1, device_id={"ctx": to}, device_id_type=MESH)
    pl.semaphore_wait(barrier, jnp.minimum(p, 2) + jnp.minimum(n - 1 - p, 2))

    def first_sends(c, carry):
        @pl.when(back2)
        def _():
            for copy in z_copy(c):
                copy.start()

        @pl.when(odd)
        def _():
            for copy in y_copy(c, (q_ref, g_ref)):
                copy.start()
        return carry

    for load in loads[:2]:
        load.wait()
    lax.fori_loop(0, chunks, first_sends, 0)

    row = lax.broadcasted_iota(jnp.int32, (BLK, HEAD), 0)
    for j in range(per):
        key_id = p * per + j
        kept = row < BLK - counts_ref[key_id]
        for d in range(3):
            for i in range(per):
                if (d == 0 and j >= i) or (d == 2 and j < i):
                    continue
                query_id = jnp.minimum((p + d) * per + i, total - 1)
                listed = jnp.int32(0)
                for slot in range(1, KPB):
                    listed = jnp.where(blocks_ref[slot, query_id] == key_id, 1, listed)
                mask[d * per + i, pl.ds(j * BLK, BLK), :] = jnp.where(
                    kept, listed.astype(jnp.float32), 0.0
                ).astype(jnp.bfloat16)

    key_row = lax.broadcasted_iota(jnp.int32, (BLK, BLK), 0)
    query_col = lax.broadcasted_iota(jnp.int32, (BLK, BLK), 1)

    dk_acc[...] = jnp.zeros_like(dk_acc)
    dv_acc[...] = jnp.zeros_like(dv_acc)
    for load in loads[2:]:
        load.wait()

    def source(d, h, i, query_ref, grad_ref):
        rows = pl.ds(i * BLK, BLK)
        cols = pl.ds(pl.multiple_of(h * HEAD, HEAD), HEAD)
        query, grad = query_ref[rows, cols], grad_ref[rows, cols]
        query_sum = None
        key_slots = {0: range(0, i + 1), 1: range(per), 2: range(i, per)}[d]
        for j in key_slots:
            at = pl.ds(j * BLK, BLK)
            key, value, allowed = k_ref[at, cols], v_ref[at, cols], None
            if d == 0 and j == i:
                limit = BLK - counts_ref[p * per + i]
                allowed = (key_row <= query_col) & (
                    (key_row < limit) | (key_row == query_col)
                )
            else:
                read = mask[d * per + i, at, :]
                key, value = key * read, value * read
            query_part, key_part, value_part = tile(query, grad, key, value, allowed)
            query_sum = query_part if query_sum is None else query_sum + query_part
            dk_acc[at, cols] += key_part
            dv_acc[at, cols] += value_part
        return query_sum * dq_scale

    def returns(c, carry):
        d1_copy(c).start()
        return carry

    def one_round(h, carry):
        @pl.when((h == heads) & has1)
        def _():
            lax.fori_loop(0, chunks - per, returns, 0)

        for i in range(per):
            rows = pl.ds(i * BLK, BLK)

            @pl.when(h < heads)
            def _():
                c = h * per + i
                cols = pl.ds(pl.multiple_of(h * HEAD, HEAD), HEAD)

                @pl.when(has2)
                def _():
                    for copy in z_copy(c):
                        copy.wait_recv()

                    @pl.when(even)
                    def _():
                        for copy in y_copy(c, (r2q, r2g)):
                            copy.start()

                    dq2[rows, cols] = source(2, h, i, r2q, r2g).astype(jnp.bfloat16)
                    d2_copy(c).start()

                dq0[rows, cols] = source(0, h, i, q_ref, g_ref)

            @pl.when((h > 0) & has1)
            def _():
                c = (h - 1) * per + i
                cols = pl.ds(pl.multiple_of((h - 1) * HEAD, HEAD), HEAD)
                for copy in y_copy(c, (q_ref, g_ref)):
                    copy.wait_recv()
                dq1[rows, cols] = source(1, h - 1, i, r1q, r1g).astype(jnp.bfloat16)

                @pl.when(h == heads)
                def _():
                    d1_copy(c).start()

        @pl.when(h > 0)
        def _():
            cols = pl.ds(pl.multiple_of((h - 1) * HEAD, HEAD), HEAD)
            dk_ref[:, cols] = (dk_acc[:, cols] * dq_scale).astype(jnp.bfloat16)
            dv_ref[:, cols] = (dv_acc[:, cols] * NORM_SCALE).astype(jnp.bfloat16)
            for store in dkv_store(h - 1):
                store.start()
        return carry

    lax.fori_loop(0, heads + 1, one_round, 0)

    def finish(c, carry):
        rows = pl.ds(pl.multiple_of(lax.rem(c, per) * BLK, BLK), BLK)
        cols = pl.ds(pl.multiple_of(lax.div(c, per) * HEAD, HEAD), HEAD)

        @pl.when(back2)
        def _():
            d2_copy(c).wait_recv()
            dq0[rows, cols] += rq2[rows, cols].astype(jnp.float32)
            for copy in z_copy(c):
                copy.wait_send()

        @pl.when(back1)
        def _():
            d1_copy(c).wait_recv()
            dq0[rows, cols] += rq1[rows, cols].astype(jnp.float32)

        dq_ref[rows, cols] = dq0[rows, cols].astype(jnp.bfloat16)
        dq_store(c).start()

        @pl.when(odd | has2)
        def _():
            for copy in y_copy(c, (q_ref, g_ref)):
                copy.wait_send()

        @pl.when(has1)
        def _():
            d1_copy(c).wait_send()

        @pl.when(has2)
        def _():
            d2_copy(c).wait_send()
        return carry

    lax.fori_loop(0, chunks, finish, 0)

    def stored(h, carry):
        for store in dkv_store(h):
            store.wait()
        for i in range(per):
            dq_store(h * per + i).wait()
        return carry

    lax.fori_loop(0, heads, stored, 0)


def near_body(n, queries, keys, values, out_grad, key_blocks, target_counts):
    rows, columns = queries.shape
    per, heads = rows // BLK, columns // HEAD
    chunks = heads * per
    narrow = pltpu.VMEM((rows, columns), jnp.bfloat16)
    wide = pltpu.VMEM((rows, columns), jnp.float32)
    pair = pltpu.SemaphoreType.DMA((2, chunks))
    single = pltpu.SemaphoreType.DMA((chunks,))
    scalars = pl.BlockSpec(memory_space=pltpu.SMEM)
    result = jax.ShapeDtypeStruct((rows, columns), jnp.bfloat16)
    return pl.pallas_call(
        functools.partial(kernel, n, per, heads),
        out_shape=(result, result, result),
        in_specs=[scalars, scalars] + [pl.BlockSpec(memory_space=pl.ANY)] * 4,
        out_specs=(pl.BlockSpec(memory_space=pl.ANY),) * 3,
        scratch_shapes=[narrow] * 15
        + [wide] * 3
        + [pltpu.VMEM((3 * per, rows, HEAD), jnp.bfloat16)]
        + [pair] * 4 + [single] * 4 + [pltpu.SemaphoreType.DMA((4,)), single, pltpu.SemaphoreType.DMA((2, heads))],
        compiler_params=pltpu.CompilerParams(
            collective_id=0, has_side_effects=True, vmem_limit_bytes=56 * 1024 * 1024
        ),
    )(key_blocks.T, target_counts, queries, out_grad, keys, values)


def from_behind(array, axis, by):
    length = lax.axis_size(axis)
    pairs = [(i, i + by) for i in range(length) if 0 <= i + by < length]
    return lax.ppermute(array, axis, pairs)


def passed_along(array, axis, by):
    length = lax.axis_size(axis)
    return lax.ppermute(array, axis, [(i, (i + by) % length) for i in range(length)])


def block_mask(query_id, key_id, target_counts):
    row_index = jnp.arange(BLK, dtype=jnp.int32)[:, None]
    col_index = jnp.arange(BLK, dtype=jnp.int32)[None, :]
    own_targets = target_counts[query_id]
    key_targets = target_counts[key_id]
    diagonal = (col_index <= row_index) & (
        (col_index < BLK - own_targets) | (col_index == row_index)
    )
    earlier = jnp.broadcast_to(col_index < BLK - key_targets, diagonal.shape)
    return jnp.where(query_id == key_id, diagonal, earlier).astype(jnp.float32)


def tile_grads(query_tile, grad_tile, key_tile, value_tile, allowed):
    head_factor = 1.0 / math.sqrt(HEAD)
    norm_scale = 1.0 / math.sqrt(KPB * BLK)
    scores = (
        jnp.einsum("ihd,jhd->hij", query_tile, key_tile, preferred_element_type=jnp.float32)
        * head_factor
    )
    sigmoid_part = jax.nn.sigmoid(scores)
    gated = allowed[None] * norm_scale
    weights = (scores * sigmoid_part * gated).astype(jnp.bfloat16)
    weight_grad = jnp.einsum(
        "ihd,jhd->hij", grad_tile, value_tile, preferred_element_type=jnp.float32
    )
    score_grad = (
        weight_grad * gated * sigmoid_part * (1.0 + scores * (1.0 - sigmoid_part))
    ).astype(jnp.bfloat16)
    query_part = (
        jnp.einsum("hij,jhd->ihd", score_grad, key_tile, preferred_element_type=jnp.float32)
        * head_factor
    )
    key_part = (
        jnp.einsum("hij,ihd->jhd", score_grad, query_tile, preferred_element_type=jnp.float32)
        * head_factor
    )
    payload_portion = jnp.einsum(
        "hij,ihd->jhd", weights, grad_tile, preferred_element_type=jnp.float32
    )
    return (query_part, key_part, payload_portion)


def visit(
    query_base,
    key_base,
    active,
    query_here,
    grad_here,
    key_here,
    value_here,
    grads,
    key_blocks,
    target_counts,
):
    per_device = query_here.shape[0]
    total_blocks = key_blocks.shape[0]

    def pair_step(pair_index, present_value):
        query_slot = pair_index // per_device
        key_slot = pair_index % per_device
        query_id = jnp.clip(query_base + query_slot, 0, total_blocks - 1)
        key_id = key_base + key_slot
        listed = active & jnp.any(key_blocks[query_id] == key_id)

        def work(accums):
            query_acc, key_acc, value_acc = accums
            safe_key = jnp.clip(key_id, 0, total_blocks - 1)
            allowed = block_mask(query_id, safe_key, target_counts)
            query_part, key_part, payload_portion = tile_grads(
                query_here[query_slot],
                grad_here[query_slot],
                key_here[key_slot],
                value_here[key_slot],
                allowed,
            )
            return (
                query_acc.at[query_slot].add(query_part),
                key_acc.at[key_slot].add(key_part),
                value_acc.at[key_slot].add(payload_portion),
            )

        return lax.cond(listed, work, lambda unchanged: unchanged, present_value)

    return lax.fori_loop(0, per_device * per_device, pair_step, grads)


def body(queries, keys, values, out_grad, key_blocks, target_counts):
    cycle_size = lax.axis_size("ctx")
    reach_hops = cycle_size // 4
    position = lax.axis_index("ctx")
    per_device = queries.shape[0] // BLK
    heads_here = queries.shape[1] // HEAD
    block_shape = (per_device, BLK, heads_here, HEAD)
    query_blocks = queries.reshape(block_shape)
    key_tiles = keys.reshape(block_shape)
    value_tiles = values.reshape(block_shape)
    grad_blocks = out_grad.reshape(block_shape)
    empty = jnp.zeros(block_shape, jnp.float32)

    def query_hop(hop_index, state):
        query_here, grad_here, query_acc, key_acc, value_acc = state
        source = position + hop_index
        query_acc, key_acc, value_acc = visit(
            source * per_device,
            position * per_device,
            source < cycle_size,
            query_here,
            grad_here,
            key_tiles,
            value_tiles,
            (query_acc, key_acc, value_acc),
            key_blocks,
            target_counts,
        )
        query_here, grad_here = from_behind((query_here, grad_here), "ctx", -1)
        query_acc = passed_along(query_acc, "ctx", -1)
        return (query_here, grad_here, query_acc, key_acc, value_acc)

    state = lax.fori_loop(
        0, reach_hops, query_hop, (query_blocks, grad_blocks, empty, empty, empty)
    )
    query_here, grad_here, query_acc, key_acc, value_acc = state
    source = position + reach_hops
    query_acc, key_acc, value_acc = visit(
        source * per_device,
        position * per_device,
        source < cycle_size,
        query_here,
        grad_here,
        key_tiles,
        value_tiles,
        (query_acc, key_acc, value_acc),
        key_blocks,
        target_counts,
    )
    query_acc = passed_along(query_acc.astype(jnp.bfloat16), "ctx", reach_hops).astype(
        query_acc.dtype
    )
    flat = queries.shape
    return (
        query_acc.reshape(flat).astype(jnp.bfloat16),
        key_acc.reshape(flat).astype(jnp.bfloat16),
        value_acc.reshape(flat).astype(jnp.bfloat16),
    )


def solution(mesh):
    in_specs = (P("ctx", "tp"), P("ctx", "tp"), P("ctx", "tp"), P("ctx", "tp"), P(), P())
    out_specs = (P("ctx", "tp"), P("ctx", "tp"), P("ctx", "tp"))
    length = mesh.shape["ctx"]
    mapped = functools.partial(near_body, length) if length // 4 == 2 else body
    return jax.shard_map(
        mapped, mesh=mesh, in_specs=in_specs, out_specs=out_specs, check_vma=False
    )
```

```python
import functools
import math

import jax
import jax.numpy as jnp
from jax import lax
from jax.experimental import pallas as pl
from jax.experimental.pallas import tpu as pltpu
from jax.sharding import PartitionSpec as P

HEAD = 128
BLK = 256
KPB = 16
MESH = pl.DeviceIdType.MESH
HEAD_FACTOR = 1.0 / math.sqrt(HEAD)
NORM_SCALE = 1.0 / math.sqrt(KPB * BLK)


def nt(a, b):
    return lax.dot_general(a, b, (((1,), (1,)), ((), ())), preferred_element_type=jnp.float32)


def tile(query, grad, key, value, key_columns, allowed=None):
    half = nt(key, query) * (0.5 * HEAD_FACTOR)
    one_tanh = 1.0 + jnp.tanh(half)
    weights = half * one_tanh
    score_grad = nt(value, grad) * (one_tanh + weights * (2.0 - one_tanh))
    if allowed is not None:
        weights = jnp.where(allowed, weights, 0.0)
        score_grad = jnp.where(allowed, score_grad, 0.0)
    weights = weights.astype(jnp.bfloat16)
    score_grad = score_grad.astype(jnp.bfloat16)
    value_part = jnp.dot(weights, grad, preferred_element_type=jnp.float32)
    key_part = jnp.dot(score_grad, query, preferred_element_type=jnp.float32)
    query_part = jnp.dot(key_columns, score_grad, preferred_element_type=jnp.float32)
    return query_part, key_part, value_part


def kernel(
    n, per, heads,
    blocks_ref, counts_ref, q_hbm, g_hbm, k_hbm, v_hbm,
    dq_hbm, dk_hbm, dv_hbm,
    dq_ref, dk_ref, dv_ref, q_ref, g_ref, k_ref, v_ref, kt_ref, r1q, r1g, r2q, r2g, dq1, dq2, rq1, rq2, dq0, dk_acc, dv_acc, mask,
    z_send, z_recv, y_send, y_recv, d1_send, d1_recv, d2_send, d2_recv, own, dq_out, dkv_out,
):
    p = lax.axis_index("ctx")
    total = n * per
    odd = lax.rem(p, 2) == 1
    even = lax.rem(p, 2) == 0
    has1, has2 = p + 1 < n, p + 2 < n
    back1, back2 = p >= 1, p >= 2
    next1, next2 = lax.rem(p + 1, n), lax.rem(p + 2, n)
    prev1, prev2 = lax.rem(p + n - 1, n), lax.rem(p + n - 2, n)
    partner = p + 1 - 2 * lax.rem(p, 2)
    chunks = heads * per
    dq_scale = 0.5 * NORM_SCALE * HEAD_FACTOR

    def part(ref, c):
        rows = pl.ds(pl.multiple_of(lax.rem(c, per) * BLK, BLK), BLK)
        cols = pl.ds(pl.multiple_of(lax.div(c, per) * HEAD, HEAD), HEAD)
        return ref.at[rows, cols]

    def remote(src, dst, c, send, recv, to):
        return pltpu.make_async_remote_copy(
            src_ref=part(src, c), dst_ref=part(dst, c),
            send_sem=send, recv_sem=recv,
            device_id={"ctx": to}, device_id_type=MESH,
        )

    def dq_store(c):
        return pltpu.make_async_copy(part(dq_ref, c), part(dq_hbm, c), dq_out.at[c])

    def dkv_store(h):
        cols = pl.ds(pl.multiple_of(h * HEAD, HEAD), HEAD)
        return [
            pltpu.make_async_copy(src.at[:, cols], dst.at[:, cols], dkv_out.at[w, h])
            for w, (src, dst) in enumerate(((dk_ref, dk_hbm), (dv_ref, dv_hbm)))
        ]

    def z_copy(c):
        return [
            remote(src, dst, c, z_send.at[w, c], z_recv.at[w, c], prev2)
            for w, (src, dst) in enumerate(((q_ref, r2q), (g_ref, r2g)))
        ]

    def y_copy(c, sources):
        return [
            remote(src, dst, c, y_send.at[w, c], y_recv.at[w, c], partner)
            for w, (src, dst) in enumerate(zip(sources, (r1q, r1g)))
        ]

    def d1_copy(c):
        return remote(dq1, rq1, c, d1_send.at[c], d1_recv.at[c], next1)

    def d2_copy(c):
        return remote(dq2, rq2, c, d2_send.at[c], d2_recv.at[c], next2)

    loads = [
        pltpu.make_async_copy(src, dst, own.at[w])
        for w, (src, dst) in enumerate(
            ((q_hbm, q_ref), (g_hbm, g_ref), (k_hbm, k_ref), (v_hbm, v_ref))
        )
    ]

    for load in loads:
        load.start()

    barrier = pltpu.get_barrier_semaphore()
    for near, to in ((back1, prev1), (back2, prev2), (has1, next1), (has2, next2)):
        @pl.when(near)
        def _():
            pl.semaphore_signal(barrier, inc=1, device_id={"ctx": to}, device_id_type=MESH)
    pl.semaphore_wait(barrier, jnp.minimum(p, 2) + jnp.minimum(n - 1 - p, 2))

    def first_sends(c, carry):
        @pl.when(back2)
        def _():
            for copy in z_copy(c):
                copy.start()

        @pl.when(odd)
        def _():
            for copy in y_copy(c, (q_ref, g_ref)):
                copy.start()
        return carry

    for load in loads[:2]:
        load.wait()
    lax.fori_loop(0, chunks, first_sends, 0)

    row = lax.broadcasted_iota(jnp.int32, (BLK, HEAD), 0)
    for j in range(per):
        key_id = p * per + j
        kept = row < BLK - counts_ref[key_id]
        for d in range(3):
            for i in range(per):
                if (d == 0 and j >= i) or (d == 2 and j < i):
                    continue
                query_id = jnp.minimum((p + d) * per + i, total - 1)
                listed = jnp.int32(0)
                for slot in range(1, KPB):
                    listed = jnp.where(blocks_ref[slot, query_id] == key_id, 1, listed)
                mask[d * per + i, pl.ds(j * BLK, BLK), :] = jnp.where(
                    kept, listed.astype(jnp.float32), 0.0
                ).astype(jnp.bfloat16)

    key_row = lax.broadcasted_iota(jnp.int32, (BLK, BLK), 0)
    query_col = lax.broadcasted_iota(jnp.int32, (BLK, BLK), 1)

    dk_acc[...] = jnp.zeros_like(dk_acc)
    dv_acc[...] = jnp.zeros_like(dv_acc)
    for load in loads[2:]:
        load.wait()
    for h in range(heads):
        cols = pl.ds(h * HEAD, HEAD)
        kt_ref[cols, :] = k_ref[:, cols].astype(jnp.float32).T.astype(jnp.bfloat16)

    def source(d, h, i, query_ref, grad_ref):
        rows = pl.ds(i * BLK, BLK)
        cols = pl.ds(pl.multiple_of(h * HEAD, HEAD), HEAD)
        query, grad = query_ref[rows, cols], grad_ref[rows, cols]
        query_sum = None
        key_slots = {0: range(0, i + 1), 1: range(per), 2: range(i, per)}[d]
        for j in key_slots:
            at = pl.ds(j * BLK, BLK)
            key, value, allowed = k_ref[at, cols], v_ref[at, cols], None
            if d == 0 and j == i:
                limit = BLK - counts_ref[p * per + i]
                allowed = (key_row <= query_col) & (
                    (key_row < limit) | (key_row == query_col)
                )
            else:
                read = mask[d * per + i, at, :]
                key, value = key * read, value * read
            query_part, key_part, value_part = tile(
                query, grad, key, value, kt_ref[cols, at], allowed
            )
            query_sum = query_part if query_sum is None else query_sum + query_part
            dk_acc[at, cols] += key_part
            dv_acc[at, cols] += value_part
        return query_sum.T * dq_scale

    def one_round(h, carry):
        for i in range(per):
            rows = pl.ds(i * BLK, BLK)

            @pl.when(h < heads)
            def _():
                c = h * per + i
                cols = pl.ds(pl.multiple_of(h * HEAD, HEAD), HEAD)

                @pl.when(has2)
                def _():
                    for copy in z_copy(c):
                        copy.wait_recv()

                    @pl.when(even)
                    def _():
                        for copy in y_copy(c, (r2q, r2g)):
                            copy.start()

                    dq2[rows, cols] = source(2, h, i, r2q, r2g).astype(jnp.bfloat16)
                    d2_copy(c).start()

                dq0[rows, cols] = source(0, h, i, q_ref, g_ref)

            @pl.when((h > 0) & has1)
            def _():
                c = (h - 1) * per + i
                cols = pl.ds(pl.multiple_of((h - 1) * HEAD, HEAD), HEAD)
                for copy in y_copy(c, (q_ref, g_ref)):
                    copy.wait_recv()
                dq1[rows, cols] = source(1, h - 1, i, r1q, r1g).astype(jnp.bfloat16)
                d1_copy(c).start()

        @pl.when(h > 0)
        def _():
            cols = pl.ds(pl.multiple_of((h - 1) * HEAD, HEAD), HEAD)
            dk_ref[:, cols] = (dk_acc[:, cols] * dq_scale).astype(jnp.bfloat16)
            dv_ref[:, cols] = (dv_acc[:, cols] * NORM_SCALE).astype(jnp.bfloat16)
            for store in dkv_store(h - 1):
                store.start()
        return carry

    lax.fori_loop(0, heads + 1, one_round, 0)

    def finish(c, carry):
        rows = pl.ds(pl.multiple_of(lax.rem(c, per) * BLK, BLK), BLK)
        cols = pl.ds(pl.multiple_of(lax.div(c, per) * HEAD, HEAD), HEAD)

        @pl.when(back2)
        def _():
            d2_copy(c).wait_recv()
            dq0[rows, cols] += rq2[rows, cols].astype(jnp.float32)
            for copy in z_copy(c):
                copy.wait_send()

        @pl.when(back1)
        def _():
            d1_copy(c).wait_recv()
            dq0[rows, cols] += rq1[rows, cols].astype(jnp.float32)

        dq_ref[rows, cols] = dq0[rows, cols].astype(jnp.bfloat16)
        dq_store(c).start()

        @pl.when(odd | has2)
        def _():
            for copy in y_copy(c, (q_ref, g_ref)):
                copy.wait_send()

        @pl.when(has1)
        def _():
            d1_copy(c).wait_send()

        @pl.when(has2)
        def _():
            d2_copy(c).wait_send()
        return carry

    lax.fori_loop(0, chunks, finish, 0)

    def stored(h, carry):
        for store in dkv_store(h):
            store.wait()
        for i in range(per):
            dq_store(h * per + i).wait()
        return carry

    lax.fori_loop(0, heads, stored, 0)


def hand_over(a_in, b_in, c_in, a_out, b_out, c_out, a, b, c, come, gone):
    half = a.shape[0] // 2
    steps = [
        (src.at[pl.ds(at, half)], held.at[pl.ds(at, half)], dst.at[pl.ds(at, half)])
        for src, held, dst in ((a_in, a, a_out), (b_in, b, b_out), (c_in, c, c_out))
        for at in (0, half)
    ]
    ins = [pltpu.make_async_copy(x, y, come.at[w]) for w, (x, y, _) in enumerate(steps)]
    outs = [pltpu.make_async_copy(y, z, gone.at[w]) for w, (_, y, z) in enumerate(steps)]
    for copy in ins:
        copy.start()
    for copy, later in zip(ins, outs):
        copy.wait()
        later.start()
    for copy in outs:
        copy.wait()


def near_body(n, queries, keys, values, out_grad, key_blocks, target_counts):
    rows, columns = queries.shape
    per, heads = rows // BLK, columns // HEAD
    chunks = heads * per
    narrow = pltpu.VMEM((rows, columns), jnp.bfloat16)
    wide = pltpu.VMEM((rows, columns), jnp.float32)
    pair = pltpu.SemaphoreType.DMA((2, chunks))
    single = pltpu.SemaphoreType.DMA((chunks,))
    scalars = pl.BlockSpec(memory_space=pltpu.SMEM)
    result = jax.ShapeDtypeStruct((rows, columns), jnp.bfloat16)
    grads = pl.pallas_call(
        functools.partial(kernel, n, per, heads),
        out_shape=(result, result, result),
        in_specs=[scalars, scalars] + [pl.BlockSpec(memory_space=pl.ANY)] * 4,
        out_specs=(pl.BlockSpec(memory_space=pl.ANY),) * 3,
        scratch_shapes=[narrow] * 7
        + [pltpu.VMEM((columns, rows), jnp.bfloat16)]
        + [narrow] * 8
        + [wide] * 3
        + [pltpu.VMEM((3 * per, rows, HEAD), jnp.bfloat16)]
        + [pair] * 4 + [single] * 4 + [pltpu.SemaphoreType.DMA((4,)), single, pltpu.SemaphoreType.DMA((2, heads))],
        compiler_params=pltpu.CompilerParams(
            collective_id=0, has_side_effects=True, vmem_limit_bytes=56 * 1024 * 1024
        ),
    )(key_blocks.T, target_counts, queries, out_grad, keys, values)
    return pl.pallas_call(
        hand_over,
        out_shape=(result, result, result),
        in_specs=[pl.BlockSpec(memory_space=pl.ANY)] * 3,
        out_specs=(pl.BlockSpec(memory_space=pl.ANY),) * 3,
        scratch_shapes=[narrow] * 3 + [pltpu.SemaphoreType.DMA((6,))] * 2,
        compiler_params=pltpu.CompilerParams(vmem_limit_bytes=56 * 1024 * 1024),
    )(*grads)


def from_behind(array, axis, by):
    length = lax.axis_size(axis)
    pairs = [(i, i + by) for i in range(length) if 0 <= i + by < length]
    return lax.ppermute(array, axis, pairs)


def passed_along(array, axis, by):
    length = lax.axis_size(axis)
    return lax.ppermute(array, axis, [(i, (i + by) % length) for i in range(length)])


def block_mask(query_id, key_id, target_counts):
    row_index = jnp.arange(BLK, dtype=jnp.int32)[:, None]
    col_index = jnp.arange(BLK, dtype=jnp.int32)[None, :]
    own_targets = target_counts[query_id]
    key_targets = target_counts[key_id]
    diagonal = (col_index <= row_index) & (
        (col_index < BLK - own_targets) | (col_index == row_index)
    )
    earlier = jnp.broadcast_to(col_index < BLK - key_targets, diagonal.shape)
    return jnp.where(query_id == key_id, diagonal, earlier).astype(jnp.float32)


def tile_grads(query_tile, grad_tile, key_tile, value_tile, allowed):
    head_factor = 1.0 / math.sqrt(HEAD)
    norm_scale = 1.0 / math.sqrt(KPB * BLK)
    scores = (
        jnp.einsum("ihd,jhd->hij", query_tile, key_tile, preferred_element_type=jnp.float32)
        * head_factor
    )
    sigmoid_part = jax.nn.sigmoid(scores)
    gated = allowed[None] * norm_scale
    weights = (scores * sigmoid_part * gated).astype(jnp.bfloat16)
    weight_grad = jnp.einsum(
        "ihd,jhd->hij", grad_tile, value_tile, preferred_element_type=jnp.float32
    )
    score_grad = (
        weight_grad * gated * sigmoid_part * (1.0 + scores * (1.0 - sigmoid_part))
    ).astype(jnp.bfloat16)
    query_part = (
        jnp.einsum("hij,jhd->ihd", score_grad, key_tile, preferred_element_type=jnp.float32)
        * head_factor
    )
    key_part = (
        jnp.einsum("hij,ihd->jhd", score_grad, query_tile, preferred_element_type=jnp.float32)
        * head_factor
    )
    payload_portion = jnp.einsum(
        "hij,ihd->jhd", weights, grad_tile, preferred_element_type=jnp.float32
    )
    return (query_part, key_part, payload_portion)


def visit(
    query_base,
    key_base,
    active,
    query_here,
    grad_here,
    key_here,
    value_here,
    grads,
    key_blocks,
    target_counts,
):
    per_device = query_here.shape[0]
    total_blocks = key_blocks.shape[0]

    def pair_step(pair_index, present_value):
        query_slot = pair_index // per_device
        key_slot = pair_index % per_device
        query_id = jnp.clip(query_base + query_slot, 0, total_blocks - 1)
        key_id = key_base + key_slot
        listed = active & jnp.any(key_blocks[query_id] == key_id)

        def work(accums):
            query_acc, key_acc, value_acc = accums
            safe_key = jnp.clip(key_id, 0, total_blocks - 1)
            allowed = block_mask(query_id, safe_key, target_counts)
            query_part, key_part, payload_portion = tile_grads(
                query_here[query_slot],
                grad_here[query_slot],
                key_here[key_slot],
                value_here[key_slot],
                allowed,
            )
            return (
                query_acc.at[query_slot].add(query_part),
                key_acc.at[key_slot].add(key_part),
                value_acc.at[key_slot].add(payload_portion),
            )

        return lax.cond(listed, work, lambda unchanged: unchanged, present_value)

    return lax.fori_loop(0, per_device * per_device, pair_step, grads)


def body(queries, keys, values, out_grad, key_blocks, target_counts):
    cycle_size = lax.axis_size("ctx")
    reach_hops = cycle_size // 4
    position = lax.axis_index("ctx")
    per_device = queries.shape[0] // BLK
    heads_here = queries.shape[1] // HEAD
    block_shape = (per_device, BLK, heads_here, HEAD)
    query_blocks = queries.reshape(block_shape)
    key_tiles = keys.reshape(block_shape)
    value_tiles = values.reshape(block_shape)
    grad_blocks = out_grad.reshape(block_shape)
    empty = jnp.zeros(block_shape, jnp.float32)

    def query_hop(hop_index, state):
        query_here, grad_here, query_acc, key_acc, value_acc = state
        source = position + hop_index
        query_acc, key_acc, value_acc = visit(
            source * per_device,
            position * per_device,
            source < cycle_size,
            query_here,
            grad_here,
            key_tiles,
            value_tiles,
            (query_acc, key_acc, value_acc),
            key_blocks,
            target_counts,
        )
        query_here, grad_here = from_behind((query_here, grad_here), "ctx", -1)
        query_acc = passed_along(query_acc, "ctx", -1)
        return (query_here, grad_here, query_acc, key_acc, value_acc)

    state = lax.fori_loop(
        0, reach_hops, query_hop, (query_blocks, grad_blocks, empty, empty, empty)
    )
    query_here, grad_here, query_acc, key_acc, value_acc = state
    source = position + reach_hops
    query_acc, key_acc, value_acc = visit(
        source * per_device,
        position * per_device,
        source < cycle_size,
        query_here,
        grad_here,
        key_tiles,
        value_tiles,
        (query_acc, key_acc, value_acc),
        key_blocks,
        target_counts,
    )
    query_acc = passed_along(query_acc.astype(jnp.bfloat16), "ctx", reach_hops).astype(
        query_acc.dtype
    )
    flat = queries.shape
    return (
        query_acc.reshape(flat).astype(jnp.bfloat16),
        key_acc.reshape(flat).astype(jnp.bfloat16),
        value_acc.reshape(flat).astype(jnp.bfloat16),
    )


def solution(mesh):
    in_specs = (P("ctx", "tp"), P("ctx", "tp"), P("ctx", "tp"), P("ctx", "tp"), P(), P())
    out_specs = (P("ctx", "tp"), P("ctx", "tp"), P("ctx", "tp"))
    length = mesh.shape["ctx"]
    mapped = functools.partial(near_body, length) if length // 4 == 2 else body
    return jax.shard_map(
        mapped, mesh=mesh, in_specs=in_specs, out_specs=out_specs, check_vma=False
    )
```

```python
import functools
import math

import jax
import jax.numpy as jnp
from jax import lax
from jax.experimental import pallas as pl
from jax.experimental.pallas import tpu as pltpu
from jax.sharding import PartitionSpec as P

HEAD = 128
BLK = 256
KPB = 16
MESH = pl.DeviceIdType.MESH
HEAD_FACTOR = 1.0 / math.sqrt(HEAD)
NORM_SCALE = 1.0 / math.sqrt(KPB * BLK)


def nt(a, b):
    return lax.dot_general(a, b, (((1,), (1,)), ((), ())), preferred_element_type=jnp.float32)


def tile(query, grad, key, value, key_columns, allowed=None):
    half = nt(key, query) * (0.5 * HEAD_FACTOR)
    one_tanh = 1.0 + jnp.tanh(half)
    weights = half * one_tanh
    score_grad = nt(value, grad) * (one_tanh + weights * (2.0 - one_tanh))
    if allowed is not None:
        weights = jnp.where(allowed, weights, 0.0)
        score_grad = jnp.where(allowed, score_grad, 0.0)
    weights = weights.astype(jnp.bfloat16)
    score_grad = score_grad.astype(jnp.bfloat16)
    value_part = jnp.dot(weights, grad, preferred_element_type=jnp.float32)
    key_part = jnp.dot(score_grad, query, preferred_element_type=jnp.float32)
    query_part = jnp.dot(key_columns, score_grad, preferred_element_type=jnp.float32)
    return query_part, key_part, value_part


def kernel(
    n, per, heads,
    blocks_ref, counts_ref, q_hbm, g_hbm, k_hbm, v_hbm,
    dq_hbm, dk_hbm, dv_hbm,
    dq_ref, dk_ref, dv_ref, qg_ref, k_ref, v_ref, kt_ref, r1, r2, dq1, dq2, rq1, rq2, dq0, dk_acc, dv_acc, mask,
    z_send, z_recv, y_send, y_recv, d1_send, d1_recv, d2_send, d2_recv, qg_own, kv_own, dq_out, dkv_out,
):
    p = lax.axis_index("ctx")
    total = n * per
    odd = lax.rem(p, 2) == 1
    even = lax.rem(p, 2) == 0
    has1, has2 = p + 1 < n, p + 2 < n
    back1, back2 = p >= 1, p >= 2
    next1, next2 = lax.rem(p + 1, n), lax.rem(p + 2, n)
    prev1, prev2 = lax.rem(p + n - 1, n), lax.rem(p + n - 2, n)
    partner = p + 1 - 2 * lax.rem(p, 2)
    chunks = heads * per
    dq_scale = 0.5 * NORM_SCALE * HEAD_FACTOR

    def part(ref, c):
        rows = pl.ds(pl.multiple_of(lax.rem(c, per) * BLK, BLK), BLK)
        cols = pl.ds(pl.multiple_of(lax.div(c, per) * HEAD, HEAD), HEAD)
        return ref.at[rows, cols]

    def columns(ref, h):
        return ref.at[:, pl.ds(pl.multiple_of(h * HEAD, HEAD), HEAD)]

    def remote(src, dst, c, send, recv, to):
        return pltpu.make_async_remote_copy(
            src_ref=src.at[c], dst_ref=dst.at[c],
            send_sem=send.at[c], recv_sem=recv.at[c],
            device_id={"ctx": to}, device_id_type=MESH,
        )

    def qg_load(c):
        return [
            pltpu.make_async_copy(
                part(src, c), qg_ref.at[c, pl.ds(w * BLK, BLK)], qg_own.at[w, c]
            )
            for w, src in enumerate((q_hbm, g_hbm))
        ]

    def kv_load(h):
        return [
            pltpu.make_async_copy(columns(src, h), dst.at[h], kv_own.at[w, h])
            for w, (src, dst) in enumerate(((k_hbm, k_ref), (v_hbm, v_ref)))
        ]

    def dq_store(c):
        return pltpu.make_async_copy(dq_ref.at[c], part(dq_hbm, c), dq_out.at[c])

    def dkv_store(h):
        return [
            pltpu.make_async_copy(src.at[h], columns(dst, h), dkv_out.at[w, h])
            for w, (src, dst) in enumerate(((dk_ref, dk_hbm), (dv_ref, dv_hbm)))
        ]

    def z_copy(c):
        return remote(qg_ref, r2, c, z_send, z_recv, prev2)

    def y_copy(c, source):
        return remote(source, r1, c, y_send, y_recv, partner)

    def d1_copy(c):
        return remote(dq1, rq1, c, d1_send, d1_recv, next1)

    def d2_copy(c):
        return remote(dq2, rq2, c, d2_send, d2_recv, next2)

    def start_qg(c, carry):
        for load in qg_load(c):
            load.start()
        return carry

    def start_kv(h, carry):
        for load in kv_load(h):
            load.start()
        return carry

    def wait_kv(h, carry):
        for load in kv_load(h):
            load.wait()
        kt_ref[h] = k_ref[h].astype(jnp.float32).T.astype(jnp.bfloat16)
        return carry

    lax.fori_loop(0, chunks, start_qg, 0)
    lax.fori_loop(0, heads, start_kv, 0)

    barrier = pltpu.get_barrier_semaphore()
    for near, to in ((back1, prev1), (back2, prev2), (has1, next1), (has2, next2)):
        @pl.when(near)
        def _():
            pl.semaphore_signal(barrier, inc=1, device_id={"ctx": to}, device_id_type=MESH)
    pl.semaphore_wait(barrier, jnp.minimum(p, 2) + jnp.minimum(n - 1 - p, 2))

    def first_sends(c, carry):
        for load in qg_load(c):
            load.wait()

        @pl.when(back2)
        def _():
            z_copy(c).start()

        @pl.when(odd)
        def _():
            y_copy(c, qg_ref).start()
        return carry

    lax.fori_loop(0, chunks, first_sends, 0)

    row = lax.broadcasted_iota(jnp.int32, (BLK, HEAD), 0)
    for j in range(per):
        key_id = p * per + j
        kept = row < BLK - counts_ref[key_id]
        for d in range(3):
            for i in range(per):
                if (d == 0 and j >= i) or (d == 2 and j < i):
                    continue
                query_id = jnp.minimum((p + d) * per + i, total - 1)
                listed = jnp.int32(0)
                for slot in range(1, KPB):
                    listed = jnp.where(blocks_ref[slot, query_id] == key_id, 1, listed)
                mask[d * per + i, pl.ds(j * BLK, BLK), :] = jnp.where(
                    kept, listed.astype(jnp.float32), 0.0
                ).astype(jnp.bfloat16)

    key_row = lax.broadcasted_iota(jnp.int32, (BLK, BLK), 0)
    query_col = lax.broadcasted_iota(jnp.int32, (BLK, BLK), 1)

    dk_acc[...] = jnp.zeros_like(dk_acc)
    dv_acc[...] = jnp.zeros_like(dv_acc)
    lax.fori_loop(0, heads, wait_kv, 0)

    def source(d, h, i, qg):
        c = h * per + i
        query, grad = qg[c, pl.ds(0, BLK), :], qg[c, pl.ds(BLK, BLK), :]
        query_sum = None
        key_slots = {0: range(0, i + 1), 1: range(per), 2: range(i, per)}[d]
        for j in key_slots:
            at = pl.ds(j * BLK, BLK)
            key, value, allowed = k_ref[h, at, :], v_ref[h, at, :], None
            if d == 0 and j == i:
                limit = BLK - counts_ref[p * per + i]
                allowed = (key_row <= query_col) & (
                    (key_row < limit) | (key_row == query_col)
                )
            else:
                read = mask[d * per + i, at, :]
                key, value = key * read, value * read
            query_part, key_part, value_part = tile(
                query, grad, key, value, kt_ref[h, :, at], allowed
            )
            query_sum = query_part if query_sum is None else query_sum + query_part
            dk_acc[h, at, :] += key_part
            dv_acc[h, at, :] += value_part
        return query_sum.T * dq_scale

    def one_round(h, carry):
        for i in range(per):
            @pl.when(h < heads)
            def _():
                c = h * per + i

                @pl.when(has2)
                def _():
                    z_copy(c).wait_recv()

                    @pl.when(even)
                    def _():
                        y_copy(c, r2).start()

                    dq2[c] = source(2, h, i, r2).astype(jnp.bfloat16)
                    d2_copy(c).start()

                dq0[c] = source(0, h, i, qg_ref)

            @pl.when((h > 0) & has1)
            def _():
                c = (h - 1) * per + i
                y_copy(c, qg_ref).wait_recv()
                dq1[c] = source(1, h - 1, i, r1).astype(jnp.bfloat16)
                d1_copy(c).start()

        @pl.when(h > 0)
        def _():
            dk_ref[h - 1] = (dk_acc[h - 1] * dq_scale).astype(jnp.bfloat16)
            dv_ref[h - 1] = (dv_acc[h - 1] * NORM_SCALE).astype(jnp.bfloat16)
            for store in dkv_store(h - 1):
                store.start()
        return carry

    lax.fori_loop(0, heads + 1, one_round, 0)

    def finish(c, carry):
        @pl.when(back2)
        def _():
            d2_copy(c).wait_recv()
            dq0[c] += rq2[c].astype(jnp.float32)
            z_copy(c).wait_send()

        @pl.when(back1)
        def _():
            d1_copy(c).wait_recv()
            dq0[c] += rq1[c].astype(jnp.float32)

        dq_ref[c] = dq0[c].astype(jnp.bfloat16)
        dq_store(c).start()

        @pl.when(odd | has2)
        def _():
            y_copy(c, qg_ref).wait_send()

        @pl.when(has1)
        def _():
            d1_copy(c).wait_send()

        @pl.when(has2)
        def _():
            d2_copy(c).wait_send()
        return carry

    lax.fori_loop(0, chunks, finish, 0)

    def stored(h, carry):
        for store in dkv_store(h):
            store.wait()
        for i in range(per):
            dq_store(h * per + i).wait()
        return carry

    lax.fori_loop(0, heads, stored, 0)


def hand_over(a_in, b_in, c_in, a_out, b_out, c_out, a, b, c, come, gone):
    half = a.shape[0] // 2
    steps = [
        (src.at[pl.ds(at, half)], held.at[pl.ds(at, half)], dst.at[pl.ds(at, half)])
        for src, held, dst in ((a_in, a, a_out), (b_in, b, b_out), (c_in, c, c_out))
        for at in (0, half)
    ]
    ins = [pltpu.make_async_copy(x, y, come.at[w]) for w, (x, y, _) in enumerate(steps)]
    outs = [pltpu.make_async_copy(y, z, gone.at[w]) for w, (_, y, z) in enumerate(steps)]
    for copy in ins:
        copy.start()
    for copy, later in zip(ins, outs):
        copy.wait()
        later.start()
    for copy in outs:
        copy.wait()


def near_body(n, queries, keys, values, out_grad, key_blocks, target_counts):
    rows, columns = queries.shape
    per, heads = rows // BLK, columns // HEAD
    chunks = heads * per
    narrow = pltpu.VMEM((rows, columns), jnp.bfloat16)
    by_chunk = pltpu.VMEM((chunks, BLK, HEAD), jnp.bfloat16)
    pairs = pltpu.VMEM((chunks, 2 * BLK, HEAD), jnp.bfloat16)
    by_head = pltpu.VMEM((heads, rows, HEAD), jnp.bfloat16)
    head_sum = pltpu.VMEM((heads, rows, HEAD), jnp.float32)
    single = pltpu.SemaphoreType.DMA((chunks,))
    scalars = pl.BlockSpec(memory_space=pltpu.SMEM)
    result = jax.ShapeDtypeStruct((rows, columns), jnp.bfloat16)
    grads = pl.pallas_call(
        functools.partial(kernel, n, per, heads),
        out_shape=(result, result, result),
        in_specs=[scalars, scalars] + [pl.BlockSpec(memory_space=pl.ANY)] * 4,
        out_specs=(pl.BlockSpec(memory_space=pl.ANY),) * 3,
        scratch_shapes=[by_chunk, by_head, by_head, pairs, by_head, by_head]
        + [pltpu.VMEM((heads, HEAD, rows), jnp.bfloat16), pairs, pairs]
        + [by_chunk] * 4
        + [pltpu.VMEM((chunks, BLK, HEAD), jnp.float32), head_sum, head_sum]
        + [pltpu.VMEM((3 * per, rows, HEAD), jnp.bfloat16)]
        + [single] * 8
        + [pltpu.SemaphoreType.DMA((2, chunks)), pltpu.SemaphoreType.DMA((2, heads))]
        + [single, pltpu.SemaphoreType.DMA((2, heads))],
        compiler_params=pltpu.CompilerParams(
            collective_id=0, has_side_effects=True, vmem_limit_bytes=56 * 1024 * 1024
        ),
    )(key_blocks.T, target_counts, queries, out_grad, keys, values)
    return pl.pallas_call(
        hand_over,
        out_shape=(result, result, result),
        in_specs=[pl.BlockSpec(memory_space=pl.ANY)] * 3,
        out_specs=(pl.BlockSpec(memory_space=pl.ANY),) * 3,
        scratch_shapes=[narrow] * 3 + [pltpu.SemaphoreType.DMA((6,))] * 2,
        compiler_params=pltpu.CompilerParams(vmem_limit_bytes=56 * 1024 * 1024),
    )(*grads)


def from_behind(array, axis, by):
    length = lax.axis_size(axis)
    pairs = [(i, i + by) for i in range(length) if 0 <= i + by < length]
    return lax.ppermute(array, axis, pairs)


def passed_along(array, axis, by):
    length = lax.axis_size(axis)
    return lax.ppermute(array, axis, [(i, (i + by) % length) for i in range(length)])


def block_mask(query_id, key_id, target_counts):
    row_index = jnp.arange(BLK, dtype=jnp.int32)[:, None]
    col_index = jnp.arange(BLK, dtype=jnp.int32)[None, :]
    own_targets = target_counts[query_id]
    key_targets = target_counts[key_id]
    diagonal = (col_index <= row_index) & (
        (col_index < BLK - own_targets) | (col_index == row_index)
    )
    earlier = jnp.broadcast_to(col_index < BLK - key_targets, diagonal.shape)
    return jnp.where(query_id == key_id, diagonal, earlier).astype(jnp.float32)


def tile_grads(query_tile, grad_tile, key_tile, value_tile, allowed):
    head_factor = 1.0 / math.sqrt(HEAD)
    norm_scale = 1.0 / math.sqrt(KPB * BLK)
    scores = (
        jnp.einsum("ihd,jhd->hij", query_tile, key_tile, preferred_element_type=jnp.float32)
        * head_factor
    )
    sigmoid_part = jax.nn.sigmoid(scores)
    gated = allowed[None] * norm_scale
    weights = (scores * sigmoid_part * gated).astype(jnp.bfloat16)
    weight_grad = jnp.einsum(
        "ihd,jhd->hij", grad_tile, value_tile, preferred_element_type=jnp.float32
    )
    score_grad = (
        weight_grad * gated * sigmoid_part * (1.0 + scores * (1.0 - sigmoid_part))
    ).astype(jnp.bfloat16)
    query_part = (
        jnp.einsum("hij,jhd->ihd", score_grad, key_tile, preferred_element_type=jnp.float32)
        * head_factor
    )
    key_part = (
        jnp.einsum("hij,ihd->jhd", score_grad, query_tile, preferred_element_type=jnp.float32)
        * head_factor
    )
    payload_portion = jnp.einsum(
        "hij,ihd->jhd", weights, grad_tile, preferred_element_type=jnp.float32
    )
    return (query_part, key_part, payload_portion)


def visit(
    query_base,
    key_base,
    active,
    query_here,
    grad_here,
    key_here,
    value_here,
    grads,
    key_blocks,
    target_counts,
):
    per_device = query_here.shape[0]
    total_blocks = key_blocks.shape[0]

    def pair_step(pair_index, present_value):
        query_slot = pair_index // per_device
        key_slot = pair_index % per_device
        query_id = jnp.clip(query_base + query_slot, 0, total_blocks - 1)
        key_id = key_base + key_slot
        listed = active & jnp.any(key_blocks[query_id] == key_id)

        def work(accums):
            query_acc, key_acc, value_acc = accums
            safe_key = jnp.clip(key_id, 0, total_blocks - 1)
            allowed = block_mask(query_id, safe_key, target_counts)
            query_part, key_part, payload_portion = tile_grads(
                query_here[query_slot],
                grad_here[query_slot],
                key_here[key_slot],
                value_here[key_slot],
                allowed,
            )
            return (
                query_acc.at[query_slot].add(query_part),
                key_acc.at[key_slot].add(key_part),
                value_acc.at[key_slot].add(payload_portion),
            )

        return lax.cond(listed, work, lambda unchanged: unchanged, present_value)

    return lax.fori_loop(0, per_device * per_device, pair_step, grads)


def body(queries, keys, values, out_grad, key_blocks, target_counts):
    cycle_size = lax.axis_size("ctx")
    reach_hops = cycle_size // 4
    position = lax.axis_index("ctx")
    per_device = queries.shape[0] // BLK
    heads_here = queries.shape[1] // HEAD
    block_shape = (per_device, BLK, heads_here, HEAD)
    query_blocks = queries.reshape(block_shape)
    key_tiles = keys.reshape(block_shape)
    value_tiles = values.reshape(block_shape)
    grad_blocks = out_grad.reshape(block_shape)
    empty = jnp.zeros(block_shape, jnp.float32)

    def query_hop(hop_index, state):
        query_here, grad_here, query_acc, key_acc, value_acc = state
        source = position + hop_index
        query_acc, key_acc, value_acc = visit(
            source * per_device,
            position * per_device,
            source < cycle_size,
            query_here,
            grad_here,
            key_tiles,
            value_tiles,
            (query_acc, key_acc, value_acc),
            key_blocks,
            target_counts,
        )
        query_here, grad_here = from_behind((query_here, grad_here), "ctx", -1)
        query_acc = passed_along(query_acc, "ctx", -1)
        return (query_here, grad_here, query_acc, key_acc, value_acc)

    state = lax.fori_loop(
        0, reach_hops, query_hop, (query_blocks, grad_blocks, empty, empty, empty)
    )
    query_here, grad_here, query_acc, key_acc, value_acc = state
    source = position + reach_hops
    query_acc, key_acc, value_acc = visit(
        source * per_device,
        position * per_device,
        source < cycle_size,
        query_here,
        grad_here,
        key_tiles,
        value_tiles,
        (query_acc, key_acc, value_acc),
        key_blocks,
        target_counts,
    )
    query_acc = passed_along(query_acc.astype(jnp.bfloat16), "ctx", reach_hops).astype(
        query_acc.dtype
    )
    flat = queries.shape
    return (
        query_acc.reshape(flat).astype(jnp.bfloat16),
        key_acc.reshape(flat).astype(jnp.bfloat16),
        value_acc.reshape(flat).astype(jnp.bfloat16),
    )


def solution(mesh):
    in_specs = (P("ctx", "tp"), P("ctx", "tp"), P("ctx", "tp"), P("ctx", "tp"), P(), P())
    out_specs = (P("ctx", "tp"), P("ctx", "tp"), P("ctx", "tp"))
    length = mesh.shape["ctx"]
    mapped = functools.partial(near_body, length) if length // 4 == 2 else body
    return jax.shard_map(
        mapped, mesh=mesh, in_specs=in_specs, out_specs=out_specs, check_vma=False
    )
```

```python
import functools
import math

import jax
import jax.numpy as jnp
from jax import lax
from jax.experimental import pallas as pl
from jax.experimental.pallas import tpu as pltpu
from jax.sharding import PartitionSpec as P

HEAD = 128
BLK = 256
KPB = 16
MESH = pl.DeviceIdType.MESH
HEAD_FACTOR = 1.0 / math.sqrt(HEAD)
NORM_SCALE = 1.0 / math.sqrt(KPB * BLK)


def nt(a, b):
    return lax.dot_general(a, b, (((1,), (1,)), ((), ())), preferred_element_type=jnp.float32)


def tile(query, grad, key, value, key_columns, allowed=None):
    half = nt(key, query) * (0.5 * HEAD_FACTOR)
    one_tanh = 1.0 + jnp.tanh(half)
    weights = half * one_tanh
    score_grad = nt(value, grad) * (one_tanh + weights * (2.0 - one_tanh))
    if allowed is not None:
        weights = jnp.where(allowed, weights, 0.0)
        score_grad = jnp.where(allowed, score_grad, 0.0)
    weights = weights.astype(jnp.bfloat16)
    score_grad = score_grad.astype(jnp.bfloat16)
    value_part = jnp.dot(weights, grad, preferred_element_type=jnp.float32)
    key_part = jnp.dot(score_grad, query, preferred_element_type=jnp.float32)
    query_part = jnp.dot(key_columns, score_grad, preferred_element_type=jnp.float32)
    return query_part, key_part, value_part


def kernel(
    n, per, heads,
    blocks_ref, counts_ref, q_hbm, g_hbm, k_hbm, v_hbm,
    dq_hbm, dk_hbm, dv_hbm,
    dq_ref, dk_ref, dv_ref, qg_ref, k_ref, v_ref, kt_ref, r1, r2, dq1, dq2, rq1, rq2, dq0, dk_new, dv_new, dk_old, dv_old, mask,
    z_send, z_recv, y_send, y_recv, d1_send, d1_recv, d2_send, d2_recv, qg_own, kv_own, dq_out, dkv_out,
):
    p = lax.axis_index("ctx")
    total = n * per
    odd = lax.rem(p, 2) == 1
    even = lax.rem(p, 2) == 0
    has1, has2 = p + 1 < n, p + 2 < n
    back1, back2 = p >= 1, p >= 2
    next1, next2 = lax.rem(p + 1, n), lax.rem(p + 2, n)
    prev1, prev2 = lax.rem(p + n - 1, n), lax.rem(p + n - 2, n)
    partner = p + 1 - 2 * lax.rem(p, 2)
    chunks = heads * per
    dq_scale = 0.5 * NORM_SCALE * HEAD_FACTOR

    def part(ref, c):
        rows = pl.ds(pl.multiple_of(lax.rem(c, per) * BLK, BLK), BLK)
        cols = pl.ds(pl.multiple_of(lax.div(c, per) * HEAD, HEAD), HEAD)
        return ref.at[rows, cols]

    def columns(ref, h):
        return ref.at[:, pl.ds(pl.multiple_of(h * HEAD, HEAD), HEAD)]

    def remote(src, dst, c, send, recv, to):
        return pltpu.make_async_remote_copy(
            src_ref=src.at[c], dst_ref=dst.at[c],
            send_sem=send.at[c], recv_sem=recv.at[c],
            device_id={"ctx": to}, device_id_type=MESH,
        )

    def qg_load(c):
        return [
            pltpu.make_async_copy(
                part(src, c), qg_ref.at[c, pl.ds(w * BLK, BLK)], qg_own.at[w, c]
            )
            for w, src in enumerate((q_hbm, g_hbm))
        ]

    def kv_load(h):
        return [
            pltpu.make_async_copy(columns(src, h), dst.at[h], kv_own.at[w, h])
            for w, (src, dst) in enumerate(((k_hbm, k_ref), (v_hbm, v_ref)))
        ]

    def dq_store(c):
        return pltpu.make_async_copy(dq_ref.at[c], part(dq_hbm, c), dq_out.at[c])

    def dkv_store(h):
        return [
            pltpu.make_async_copy(src.at[h], columns(dst, h), dkv_out.at[w, h])
            for w, (src, dst) in enumerate(((dk_ref, dk_hbm), (dv_ref, dv_hbm)))
        ]

    def z_copy(c):
        return remote(qg_ref, r2, c, z_send, z_recv, prev2)

    def y_copy(c, source):
        return remote(source, r1, c, y_send, y_recv, partner)

    def d1_copy(c):
        return remote(dq1, rq1, c, d1_send, d1_recv, next1)

    def d2_copy(c):
        return remote(dq2, rq2, c, d2_send, d2_recv, next2)

    def start_qg(c, carry):
        for load in qg_load(c):
            load.start()
        return carry

    def start_kv(h, carry):
        for load in kv_load(h):
            load.start()
        return carry

    def wait_kv(h, carry):
        for load in kv_load(h):
            load.wait()
        kt_ref[h] = k_ref[h].astype(jnp.float32).T.astype(jnp.bfloat16)
        return carry

    lax.fori_loop(0, chunks, start_qg, 0)
    lax.fori_loop(0, heads, start_kv, 0)

    barrier = pltpu.get_barrier_semaphore()
    for near, to in ((back1, prev1), (back2, prev2), (has1, next1), (has2, next2)):
        @pl.when(near)
        def _():
            pl.semaphore_signal(barrier, inc=1, device_id={"ctx": to}, device_id_type=MESH)
    pl.semaphore_wait(barrier, jnp.minimum(p, 2) + jnp.minimum(n - 1 - p, 2))

    def first_sends(c, carry):
        for load in qg_load(c):
            load.wait()

        @pl.when(back2)
        def _():
            z_copy(c).start()

        @pl.when(odd)
        def _():
            y_copy(c, qg_ref).start()
        return carry

    lax.fori_loop(0, chunks, first_sends, 0)

    row = lax.broadcasted_iota(jnp.int32, (BLK, HEAD), 0)
    for j in range(per):
        key_id = p * per + j
        kept = row < BLK - counts_ref[key_id]
        for d in range(3):
            for i in range(per):
                if (d == 0 and j >= i) or (d == 2 and j < i):
                    continue
                query_id = jnp.minimum((p + d) * per + i, total - 1)
                listed = jnp.int32(0)
                for slot in range(1, KPB):
                    listed = jnp.where(blocks_ref[slot, query_id] == key_id, 1, listed)
                mask[d * per + i, pl.ds(j * BLK, BLK), :] = jnp.where(
                    kept, listed.astype(jnp.float32), 0.0
                ).astype(jnp.bfloat16)

    key_row = lax.broadcasted_iota(jnp.int32, (BLK, BLK), 0)
    query_col = lax.broadcasted_iota(jnp.int32, (BLK, BLK), 1)

    dk_new[...] = jnp.zeros_like(dk_new)
    dv_new[...] = jnp.zeros_like(dv_new)
    lax.fori_loop(0, heads, wait_kv, 0)

    def source(d, h, i, qg, dk_sum, dv_sum):
        c = h * per + i
        query, grad = qg[c, pl.ds(0, BLK), :], qg[c, pl.ds(BLK, BLK), :]
        query_sum = None
        key_slots = {0: range(0, i + 1), 1: range(per), 2: range(i, per)}[d]
        for j in key_slots:
            at = pl.ds(j * BLK, BLK)
            key, value, allowed = k_ref[h, at, :], v_ref[h, at, :], None
            if d == 0 and j == i:
                limit = BLK - counts_ref[p * per + i]
                allowed = (key_row <= query_col) & (
                    (key_row < limit) | (key_row == query_col)
                )
            else:
                read = mask[d * per + i, at, :]
                key, value = key * read, value * read
            query_part, key_part, value_part = tile(
                query, grad, key, value, kt_ref[h, :, at], allowed
            )
            query_sum = query_part if query_sum is None else query_sum + query_part
            dk_sum[at, :] += key_part
            dv_sum[at, :] += value_part
        return query_sum.T * dq_scale

    def one_round(h, carry):
        for i in range(per):
            @pl.when(h < heads)
            def _():
                c = h * per + i

                @pl.when(has2)
                def _():
                    z_copy(c).wait_recv()

                    @pl.when(even)
                    def _():
                        y_copy(c, r2).start()

                    dq2[c] = source(2, h, i, r2, dk_new, dv_new).astype(jnp.bfloat16)
                    d2_copy(c).start()

                dq0[c] = source(0, h, i, qg_ref, dk_new, dv_new)

            @pl.when((h > 0) & has1)
            def _():
                c = (h - 1) * per + i
                y_copy(c, qg_ref).wait_recv()
                part_sum = source(1, h - 1, i, r1, dk_old, dv_old)
                dq1[c] = part_sum.astype(jnp.bfloat16)
                d1_copy(c).start()

        @pl.when(h > 0)
        def _():
            dk_ref[h - 1] = (dk_old[...] * dq_scale).astype(jnp.bfloat16)
            dv_ref[h - 1] = (dv_old[...] * NORM_SCALE).astype(jnp.bfloat16)
            for store in dkv_store(h - 1):
                store.start()

        dk_old[...] = dk_new[...]
        dv_old[...] = dv_new[...]
        dk_new[...] = jnp.zeros_like(dk_new)
        dv_new[...] = jnp.zeros_like(dv_new)
        return carry

    lax.fori_loop(0, heads + 1, one_round, 0)

    def finish(c, carry):
        @pl.when(back2)
        def _():
            d2_copy(c).wait_recv()
            dq0[c] += rq2[c].astype(jnp.float32)
            z_copy(c).wait_send()

        @pl.when(back1)
        def _():
            d1_copy(c).wait_recv()
            dq0[c] += rq1[c].astype(jnp.float32)

        dq_ref[c] = dq0[c].astype(jnp.bfloat16)
        dq_store(c).start()

        @pl.when(odd | has2)
        def _():
            y_copy(c, qg_ref).wait_send()

        @pl.when(has1)
        def _():
            d1_copy(c).wait_send()

        @pl.when(has2)
        def _():
            d2_copy(c).wait_send()
        return carry

    lax.fori_loop(0, chunks, finish, 0)

    def stored(h, carry):
        for store in dkv_store(h):
            store.wait()
        for i in range(per):
            dq_store(h * per + i).wait()
        return carry

    lax.fori_loop(0, heads, stored, 0)


def hand_over(a_in, b_in, c_in, a_out, b_out, c_out, a, b, c, come, gone):
    half = a.shape[0] // 2
    steps = [
        (src.at[pl.ds(at, half)], held.at[pl.ds(at, half)], dst.at[pl.ds(at, half)])
        for src, held, dst in ((a_in, a, a_out), (b_in, b, b_out), (c_in, c, c_out))
        for at in (0, half)
    ]
    ins = [pltpu.make_async_copy(x, y, come.at[w]) for w, (x, y, _) in enumerate(steps)]
    outs = [pltpu.make_async_copy(y, z, gone.at[w]) for w, (_, y, z) in enumerate(steps)]
    for copy in ins:
        copy.start()
    for copy, later in zip(ins, outs):
        copy.wait()
        later.start()
    for copy in outs:
        copy.wait()


def near_body(n, queries, keys, values, out_grad, key_blocks, target_counts):
    rows, columns = queries.shape
    per, heads = rows // BLK, columns // HEAD
    chunks = heads * per
    narrow = pltpu.VMEM((rows, columns), jnp.bfloat16)
    by_chunk = pltpu.VMEM((chunks, BLK, HEAD), jnp.bfloat16)
    pairs = pltpu.VMEM((chunks, 2 * BLK, HEAD), jnp.bfloat16)
    by_head = pltpu.VMEM((heads, rows, HEAD), jnp.bfloat16)
    head_sum = pltpu.VMEM((rows, HEAD), jnp.float32)
    single = pltpu.SemaphoreType.DMA((chunks,))
    scalars = pl.BlockSpec(memory_space=pltpu.SMEM)
    result = jax.ShapeDtypeStruct((rows, columns), jnp.bfloat16)
    grads = pl.pallas_call(
        functools.partial(kernel, n, per, heads),
        out_shape=(result, result, result),
        in_specs=[scalars, scalars] + [pl.BlockSpec(memory_space=pl.ANY)] * 4,
        out_specs=(pl.BlockSpec(memory_space=pl.ANY),) * 3,
        scratch_shapes=[by_chunk, by_head, by_head, pairs, by_head, by_head]
        + [pltpu.VMEM((heads, HEAD, rows), jnp.bfloat16), pairs, pairs]
        + [by_chunk] * 4
        + [pltpu.VMEM((chunks, BLK, HEAD), jnp.float32)]
        + [head_sum] * 4
        + [pltpu.VMEM((3 * per, rows, HEAD), jnp.bfloat16)]
        + [single] * 8
        + [pltpu.SemaphoreType.DMA((2, chunks)), pltpu.SemaphoreType.DMA((2, heads))]
        + [single, pltpu.SemaphoreType.DMA((2, heads))],
        compiler_params=pltpu.CompilerParams(
            collective_id=0, has_side_effects=True, vmem_limit_bytes=56 * 1024 * 1024
        ),
    )(key_blocks.T, target_counts, queries, out_grad, keys, values)
    return pl.pallas_call(
        hand_over,
        out_shape=(result, result, result),
        in_specs=[pl.BlockSpec(memory_space=pl.ANY)] * 3,
        out_specs=(pl.BlockSpec(memory_space=pl.ANY),) * 3,
        scratch_shapes=[narrow] * 3 + [pltpu.SemaphoreType.DMA((6,))] * 2,
        compiler_params=pltpu.CompilerParams(vmem_limit_bytes=56 * 1024 * 1024),
    )(*grads)


def from_behind(array, axis, by):
    length = lax.axis_size(axis)
    pairs = [(i, i + by) for i in range(length) if 0 <= i + by < length]
    return lax.ppermute(array, axis, pairs)


def passed_along(array, axis, by):
    length = lax.axis_size(axis)
    return lax.ppermute(array, axis, [(i, (i + by) % length) for i in range(length)])


def block_mask(query_id, key_id, target_counts):
    row_index = jnp.arange(BLK, dtype=jnp.int32)[:, None]
    col_index = jnp.arange(BLK, dtype=jnp.int32)[None, :]
    own_targets = target_counts[query_id]
    key_targets = target_counts[key_id]
    diagonal = (col_index <= row_index) & (
        (col_index < BLK - own_targets) | (col_index == row_index)
    )
    earlier = jnp.broadcast_to(col_index < BLK - key_targets, diagonal.shape)
    return jnp.where(query_id == key_id, diagonal, earlier).astype(jnp.float32)


def tile_grads(query_tile, grad_tile, key_tile, value_tile, allowed):
    head_factor = 1.0 / math.sqrt(HEAD)
    norm_scale = 1.0 / math.sqrt(KPB * BLK)
    scores = (
        jnp.einsum("ihd,jhd->hij", query_tile, key_tile, preferred_element_type=jnp.float32)
        * head_factor
    )
    sigmoid_part = jax.nn.sigmoid(scores)
    gated = allowed[None] * norm_scale
    weights = (scores * sigmoid_part * gated).astype(jnp.bfloat16)
    weight_grad = jnp.einsum(
        "ihd,jhd->hij", grad_tile, value_tile, preferred_element_type=jnp.float32
    )
    score_grad = (
        weight_grad * gated * sigmoid_part * (1.0 + scores * (1.0 - sigmoid_part))
    ).astype(jnp.bfloat16)
    query_part = (
        jnp.einsum("hij,jhd->ihd", score_grad, key_tile, preferred_element_type=jnp.float32)
        * head_factor
    )
    key_part = (
        jnp.einsum("hij,ihd->jhd", score_grad, query_tile, preferred_element_type=jnp.float32)
        * head_factor
    )
    payload_portion = jnp.einsum(
        "hij,ihd->jhd", weights, grad_tile, preferred_element_type=jnp.float32
    )
    return (query_part, key_part, payload_portion)


def visit(
    query_base,
    key_base,
    active,
    query_here,
    grad_here,
    key_here,
    value_here,
    grads,
    key_blocks,
    target_counts,
):
    per_device = query_here.shape[0]
    total_blocks = key_blocks.shape[0]

    def pair_step(pair_index, present_value):
        query_slot = pair_index // per_device
        key_slot = pair_index % per_device
        query_id = jnp.clip(query_base + query_slot, 0, total_blocks - 1)
        key_id = key_base + key_slot
        listed = active & jnp.any(key_blocks[query_id] == key_id)

        def work(accums):
            query_acc, key_acc, value_acc = accums
            safe_key = jnp.clip(key_id, 0, total_blocks - 1)
            allowed = block_mask(query_id, safe_key, target_counts)
            query_part, key_part, payload_portion = tile_grads(
                query_here[query_slot],
                grad_here[query_slot],
                key_here[key_slot],
                value_here[key_slot],
                allowed,
            )
            return (
                query_acc.at[query_slot].add(query_part),
                key_acc.at[key_slot].add(key_part),
                value_acc.at[key_slot].add(payload_portion),
            )

        return lax.cond(listed, work, lambda unchanged: unchanged, present_value)

    return lax.fori_loop(0, per_device * per_device, pair_step, grads)


def body(queries, keys, values, out_grad, key_blocks, target_counts):
    cycle_size = lax.axis_size("ctx")
    reach_hops = cycle_size // 4
    position = lax.axis_index("ctx")
    per_device = queries.shape[0] // BLK
    heads_here = queries.shape[1] // HEAD
    block_shape = (per_device, BLK, heads_here, HEAD)
    query_blocks = queries.reshape(block_shape)
    key_tiles = keys.reshape(block_shape)
    value_tiles = values.reshape(block_shape)
    grad_blocks = out_grad.reshape(block_shape)
    empty = jnp.zeros(block_shape, jnp.float32)

    def query_hop(hop_index, state):
        query_here, grad_here, query_acc, key_acc, value_acc = state
        source = position + hop_index
        query_acc, key_acc, value_acc = visit(
            source * per_device,
            position * per_device,
            source < cycle_size,
            query_here,
            grad_here,
            key_tiles,
            value_tiles,
            (query_acc, key_acc, value_acc),
            key_blocks,
            target_counts,
        )
        query_here, grad_here = from_behind((query_here, grad_here), "ctx", -1)
        query_acc = passed_along(query_acc, "ctx", -1)
        return (query_here, grad_here, query_acc, key_acc, value_acc)

    state = lax.fori_loop(
        0, reach_hops, query_hop, (query_blocks, grad_blocks, empty, empty, empty)
    )
    query_here, grad_here, query_acc, key_acc, value_acc = state
    source = position + reach_hops
    query_acc, key_acc, value_acc = visit(
        source * per_device,
        position * per_device,
        source < cycle_size,
        query_here,
        grad_here,
        key_tiles,
        value_tiles,
        (query_acc, key_acc, value_acc),
        key_blocks,
        target_counts,
    )
    query_acc = passed_along(query_acc.astype(jnp.bfloat16), "ctx", reach_hops).astype(
        query_acc.dtype
    )
    flat = queries.shape
    return (
        query_acc.reshape(flat).astype(jnp.bfloat16),
        key_acc.reshape(flat).astype(jnp.bfloat16),
        value_acc.reshape(flat).astype(jnp.bfloat16),
    )


def solution(mesh):
    in_specs = (P("ctx", "tp"), P("ctx", "tp"), P("ctx", "tp"), P("ctx", "tp"), P(), P())
    out_specs = (P("ctx", "tp"), P("ctx", "tp"), P("ctx", "tp"))
    length = mesh.shape["ctx"]
    mapped = functools.partial(near_body, length) if length // 4 == 2 else body
    return jax.shard_map(
        mapped, mesh=mesh, in_specs=in_specs, out_specs=out_specs, check_vma=False
    )
```

```python
import functools
import math

import jax
import jax.numpy as jnp
from jax import lax
from jax.experimental import pallas as pl
from jax.experimental.pallas import tpu as pltpu
from jax.sharding import PartitionSpec as P

HEAD = 128
BLK = 256
KPB = 16
MESH = pl.DeviceIdType.MESH
HEAD_FACTOR = 1.0 / math.sqrt(HEAD)
NORM_SCALE = 1.0 / math.sqrt(KPB * BLK)


def nt(a, b):
    return lax.dot_general(a, b, (((1,), (1,)), ((), ())), preferred_element_type=jnp.float32)


def tile(query, grad, key, value, key_columns, allowed=None):
    half = nt(key, query) * (0.5 * HEAD_FACTOR)
    one_tanh = 1.0 + jnp.tanh(half)
    weights = half * one_tanh
    score_grad = nt(value, grad) * (one_tanh + weights * (2.0 - one_tanh))
    if allowed is not None:
        weights = jnp.where(allowed, weights, 0.0)
        score_grad = jnp.where(allowed, score_grad, 0.0)
    weights = weights.astype(jnp.bfloat16)
    score_grad = score_grad.astype(jnp.bfloat16)
    value_part = jnp.dot(weights, grad, preferred_element_type=jnp.float32)
    key_part = jnp.dot(score_grad, query, preferred_element_type=jnp.float32)
    query_part = jnp.dot(key_columns, score_grad, preferred_element_type=jnp.float32)
    return query_part, key_part, value_part


def kernel(
    n, per, heads,
    blocks_ref, counts_ref, q_hbm, g_hbm, k_hbm, v_hbm,
    dq_hbm, dk_hbm, dv_hbm,
    dq_ref, dk_ref, dv_ref, qg_ref, k_ref, v_ref, kt_ref, r1, r2, dq1, dq2, rq1, rq2, dq0, dk_new, dv_new, dk_old, dv_old, mask,
    z_send, z_recv, y_send, y_recv, d1_send, d1_recv, d2_send, d2_recv, qg_own, kv_own, dq_out, dkv_out,
):
    p = lax.axis_index("ctx")
    total = n * per
    odd = lax.rem(p, 2) == 1
    even = lax.rem(p, 2) == 0
    has1, has2 = p + 1 < n, p + 2 < n
    back1, back2 = p >= 1, p >= 2
    next1, next2 = lax.rem(p + 1, n), lax.rem(p + 2, n)
    prev1, prev2 = lax.rem(p + n - 1, n), lax.rem(p + n - 2, n)
    partner = p + 1 - 2 * lax.rem(p, 2)
    first_core = lax.rem(lax.axis_index("tp"), 2) == 0
    second_core = lax.rem(lax.axis_index("tp"), 2) == 1
    chunks = heads * per
    lead = min(4, chunks)
    dq_scale = 0.5 * NORM_SCALE * HEAD_FACTOR

    def part(ref, c):
        rows = pl.ds(pl.multiple_of(lax.rem(c, per) * BLK, BLK), BLK)
        cols = pl.ds(pl.multiple_of(lax.div(c, per) * HEAD, HEAD), HEAD)
        return ref.at[rows, cols]

    def columns(ref, h):
        return ref.at[:, pl.ds(pl.multiple_of(h * HEAD, HEAD), HEAD)]

    def remote(src, dst, c, send, recv, to):
        return pltpu.make_async_remote_copy(
            src_ref=src.at[c], dst_ref=dst.at[c],
            send_sem=send.at[c], recv_sem=recv.at[c],
            device_id={"ctx": to}, device_id_type=MESH,
        )

    def qg_load(c):
        return [
            pltpu.make_async_copy(
                part(src, c), qg_ref.at[c, pl.ds(w * BLK, BLK)], qg_own.at[w, c]
            )
            for w, src in enumerate((q_hbm, g_hbm))
        ]

    def kv_load(h):
        return [
            pltpu.make_async_copy(columns(src, h), dst.at[h], kv_own.at[w, h])
            for w, (src, dst) in enumerate(((k_hbm, k_ref), (v_hbm, v_ref)))
        ]

    def dq_store(c):
        return pltpu.make_async_copy(dq_ref.at[c], part(dq_hbm, c), dq_out.at[c])

    def dkv_store(h):
        return [
            pltpu.make_async_copy(src.at[h], columns(dst, h), dkv_out.at[w, h])
            for w, (src, dst) in enumerate(((dk_ref, dk_hbm), (dv_ref, dv_hbm)))
        ]

    def z_copy(c):
        return remote(qg_ref, r2, c, z_send, z_recv, prev2)

    def y_copy(c, source):
        return remote(source, r1, c, y_send, y_recv, partner)

    def d1_copy(c):
        return remote(dq1, rq1, c, d1_send, d1_recv, next1)

    def d2_copy(c):
        return remote(dq2, rq2, c, d2_send, d2_recv, next2)

    def start_qg(c, carry):
        for load in qg_load(c):
            load.start()
        return carry

    def start_kv(h, carry):
        for load in kv_load(h):
            load.start()
        return carry

    def wait_kv(h, carry):
        for load in kv_load(h):
            load.wait()
        kt_ref[h] = k_ref[h].astype(jnp.float32).T.astype(jnp.bfloat16)
        return carry

    lax.fori_loop(0, chunks, start_qg, 0)
    lax.fori_loop(0, heads, start_kv, 0)

    barrier = pltpu.get_barrier_semaphore()
    for near, to in ((back1, prev1), (back2, prev2), (has1, next1), (has2, next2)):
        @pl.when(near)
        def _():
            pl.semaphore_signal(barrier, inc=1, device_id={"ctx": to}, device_id_type=MESH)
    pl.semaphore_wait(barrier, jnp.minimum(p, 2) + jnp.minimum(n - 1 - p, 2))

    def own_sends(c):
        @pl.when(back2 & first_core)
        def _():
            z_copy(c).start()

        @pl.when(odd)
        def _():
            y_copy(c, qg_ref).start()

        @pl.when(back2 & second_core)
        def _():
            z_copy(c).start()

    def loaded(c, carry):
        for load in qg_load(c):
            load.wait()
        return carry

    def first_sends(c, carry):
        loaded(c, carry)
        own_sends(c)
        return carry

    lax.fori_loop(0, lead, first_sends, 0)
    lax.fori_loop(lead, chunks, loaded, 0)

    row = lax.broadcasted_iota(jnp.int32, (BLK, HEAD), 0)
    for j in range(per):
        key_id = p * per + j
        kept = row < BLK - counts_ref[key_id]
        for d in range(3):
            for i in range(per):
                if (d == 0 and j >= i) or (d == 2 and j < i):
                    continue
                query_id = jnp.minimum((p + d) * per + i, total - 1)
                listed = jnp.int32(0)
                for slot in range(1, KPB):
                    listed = jnp.where(blocks_ref[slot, query_id] == key_id, 1, listed)
                mask[d * per + i, pl.ds(j * BLK, BLK), :] = jnp.where(
                    kept, listed.astype(jnp.float32), 0.0
                ).astype(jnp.bfloat16)

    key_row = lax.broadcasted_iota(jnp.int32, (BLK, BLK), 0)
    query_col = lax.broadcasted_iota(jnp.int32, (BLK, BLK), 1)

    dk_new[...] = jnp.zeros_like(dk_new)
    dv_new[...] = jnp.zeros_like(dv_new)
    lax.fori_loop(0, heads, wait_kv, 0)

    def source(d, h, i, qg, dk_sum, dv_sum):
        c = h * per + i
        query, grad = qg[c, pl.ds(0, BLK), :], qg[c, pl.ds(BLK, BLK), :]
        query_sum = None
        key_slots = {0: range(0, i + 1), 1: range(per), 2: range(i, per)}[d]
        for j in key_slots:
            at = pl.ds(j * BLK, BLK)
            key, value, allowed = k_ref[h, at, :], v_ref[h, at, :], None
            if d == 0 and j == i:
                limit = BLK - counts_ref[p * per + i]
                allowed = (key_row <= query_col) & (
                    (key_row < limit) | (key_row == query_col)
                )
            else:
                read = mask[d * per + i, at, :]
                key, value = key * read, value * read
            query_part, key_part, value_part = tile(
                query, grad, key, value, kt_ref[h, :, at], allowed
            )
            query_sum = query_part if query_sum is None else query_sum + query_part
            dk_sum[at, :] += key_part
            dv_sum[at, :] += value_part
        return query_sum.T * dq_scale

    def one_round(h, carry):
        for i in range(per):
            @pl.when(h < heads)
            def _():
                c = h * per + i
                more = c + lead < chunks

                @pl.when(more & first_core)
                def _():
                    own_sends(c + lead)

                @pl.when(has2)
                def _():
                    z_copy(c).wait_recv()

                    @pl.when(even)
                    def _():
                        y_copy(c, r2).start()

                @pl.when(more & second_core)
                def _():
                    own_sends(c + lead)

                @pl.when(has2)
                def _():
                    dq2[c] = source(2, h, i, r2, dk_new, dv_new).astype(jnp.bfloat16)
                    d2_copy(c).start()

                dq0[c] = source(0, h, i, qg_ref, dk_new, dv_new)

            @pl.when((h > 0) & has1)
            def _():
                c = (h - 1) * per + i
                y_copy(c, qg_ref).wait_recv()
                part_sum = source(1, h - 1, i, r1, dk_old, dv_old)
                dq1[c] = part_sum.astype(jnp.bfloat16)
                d1_copy(c).start()

        @pl.when(h > 0)
        def _():
            dk_ref[h - 1] = (dk_old[...] * dq_scale).astype(jnp.bfloat16)
            dv_ref[h - 1] = (dv_old[...] * NORM_SCALE).astype(jnp.bfloat16)
            for store in dkv_store(h - 1):
                store.start()

        dk_old[...] = dk_new[...]
        dv_old[...] = dv_new[...]
        dk_new[...] = jnp.zeros_like(dk_new)
        dv_new[...] = jnp.zeros_like(dv_new)
        return carry

    lax.fori_loop(0, heads + 1, one_round, 0)

    def finish(c, carry):
        @pl.when(back2)
        def _():
            d2_copy(c).wait_recv()
            dq0[c] += rq2[c].astype(jnp.float32)
            z_copy(c).wait_send()

        @pl.when(back1)
        def _():
            d1_copy(c).wait_recv()
            dq0[c] += rq1[c].astype(jnp.float32)

        dq_ref[c] = dq0[c].astype(jnp.bfloat16)
        dq_store(c).start()

        @pl.when(odd | has2)
        def _():
            y_copy(c, qg_ref).wait_send()

        @pl.when(has1)
        def _():
            d1_copy(c).wait_send()

        @pl.when(has2)
        def _():
            d2_copy(c).wait_send()
        return carry

    lax.fori_loop(0, chunks, finish, 0)

    def stored(h, carry):
        for store in dkv_store(h):
            store.wait()
        for i in range(per):
            dq_store(h * per + i).wait()
        return carry

    lax.fori_loop(0, heads, stored, 0)


def hand_over(a_in, b_in, c_in, a_out, b_out, c_out, a, b, c, come, gone):
    half = a.shape[0] // 2
    steps = [
        (src.at[pl.ds(at, half)], held.at[pl.ds(at, half)], dst.at[pl.ds(at, half)])
        for src, held, dst in ((a_in, a, a_out), (b_in, b, b_out), (c_in, c, c_out))
        for at in (0, half)
    ]
    ins = [pltpu.make_async_copy(x, y, come.at[w]) for w, (x, y, _) in enumerate(steps)]
    outs = [pltpu.make_async_copy(y, z, gone.at[w]) for w, (_, y, z) in enumerate(steps)]
    for copy in ins:
        copy.start()
    for copy, later in zip(ins, outs):
        copy.wait()
        later.start()
    for copy in outs:
        copy.wait()


def near_body(n, queries, keys, values, out_grad, key_blocks, target_counts):
    rows, columns = queries.shape
    per, heads = rows // BLK, columns // HEAD
    chunks = heads * per
    narrow = pltpu.VMEM((rows, columns), jnp.bfloat16)
    by_chunk = pltpu.VMEM((chunks, BLK, HEAD), jnp.bfloat16)
    pairs = pltpu.VMEM((chunks, 2 * BLK, HEAD), jnp.bfloat16)
    by_head = pltpu.VMEM((heads, rows, HEAD), jnp.bfloat16)
    head_sum = pltpu.VMEM((rows, HEAD), jnp.float32)
    single = pltpu.SemaphoreType.DMA((chunks,))
    scalars = pl.BlockSpec(memory_space=pltpu.SMEM)
    result = jax.ShapeDtypeStruct((rows, columns), jnp.bfloat16)
    grads = pl.pallas_call(
        functools.partial(kernel, n, per, heads),
        out_shape=(result, result, result),
        in_specs=[scalars, scalars] + [pl.BlockSpec(memory_space=pl.ANY)] * 4,
        out_specs=(pl.BlockSpec(memory_space=pl.ANY),) * 3,
        scratch_shapes=[by_chunk, by_head, by_head, pairs, by_head, by_head]
        + [pltpu.VMEM((heads, HEAD, rows), jnp.bfloat16), pairs, pairs]
        + [by_chunk] * 4
        + [pltpu.VMEM((chunks, BLK, HEAD), jnp.float32)]
        + [head_sum] * 4
        + [pltpu.VMEM((3 * per, rows, HEAD), jnp.bfloat16)]
        + [single] * 8
        + [pltpu.SemaphoreType.DMA((2, chunks)), pltpu.SemaphoreType.DMA((2, heads))]
        + [single, pltpu.SemaphoreType.DMA((2, heads))],
        compiler_params=pltpu.CompilerParams(
            collective_id=0, has_side_effects=True, vmem_limit_bytes=56 * 1024 * 1024
        ),
    )(key_blocks.T, target_counts, queries, out_grad, keys, values)
    return pl.pallas_call(
        hand_over,
        out_shape=(result, result, result),
        in_specs=[pl.BlockSpec(memory_space=pl.ANY)] * 3,
        out_specs=(pl.BlockSpec(memory_space=pl.ANY),) * 3,
        scratch_shapes=[narrow] * 3 + [pltpu.SemaphoreType.DMA((6,))] * 2,
        compiler_params=pltpu.CompilerParams(vmem_limit_bytes=56 * 1024 * 1024),
    )(*grads)


def from_behind(array, axis, by):
    length = lax.axis_size(axis)
    pairs = [(i, i + by) for i in range(length) if 0 <= i + by < length]
    return lax.ppermute(array, axis, pairs)


def passed_along(array, axis, by):
    length = lax.axis_size(axis)
    return lax.ppermute(array, axis, [(i, (i + by) % length) for i in range(length)])


def block_mask(query_id, key_id, target_counts):
    row_index = jnp.arange(BLK, dtype=jnp.int32)[:, None]
    col_index = jnp.arange(BLK, dtype=jnp.int32)[None, :]
    own_targets = target_counts[query_id]
    key_targets = target_counts[key_id]
    diagonal = (col_index <= row_index) & (
        (col_index < BLK - own_targets) | (col_index == row_index)
    )
    earlier = jnp.broadcast_to(col_index < BLK - key_targets, diagonal.shape)
    return jnp.where(query_id == key_id, diagonal, earlier).astype(jnp.float32)


def tile_grads(query_tile, grad_tile, key_tile, value_tile, allowed):
    head_factor = 1.0 / math.sqrt(HEAD)
    norm_scale = 1.0 / math.sqrt(KPB * BLK)
    scores = (
        jnp.einsum("ihd,jhd->hij", query_tile, key_tile, preferred_element_type=jnp.float32)
        * head_factor
    )
    sigmoid_part = jax.nn.sigmoid(scores)
    gated = allowed[None] * norm_scale
    weights = (scores * sigmoid_part * gated).astype(jnp.bfloat16)
    weight_grad = jnp.einsum(
        "ihd,jhd->hij", grad_tile, value_tile, preferred_element_type=jnp.float32
    )
    score_grad = (
        weight_grad * gated * sigmoid_part * (1.0 + scores * (1.0 - sigmoid_part))
    ).astype(jnp.bfloat16)
    query_part = (
        jnp.einsum("hij,jhd->ihd", score_grad, key_tile, preferred_element_type=jnp.float32)
        * head_factor
    )
    key_part = (
        jnp.einsum("hij,ihd->jhd", score_grad, query_tile, preferred_element_type=jnp.float32)
        * head_factor
    )
    payload_portion = jnp.einsum(
        "hij,ihd->jhd", weights, grad_tile, preferred_element_type=jnp.float32
    )
    return (query_part, key_part, payload_portion)


def visit(
    query_base,
    key_base,
    active,
    query_here,
    grad_here,
    key_here,
    value_here,
    grads,
    key_blocks,
    target_counts,
):
    per_device = query_here.shape[0]
    total_blocks = key_blocks.shape[0]

    def pair_step(pair_index, present_value):
        query_slot = pair_index // per_device
        key_slot = pair_index % per_device
        query_id = jnp.clip(query_base + query_slot, 0, total_blocks - 1)
        key_id = key_base + key_slot
        listed = active & jnp.any(key_blocks[query_id] == key_id)

        def work(accums):
            query_acc, key_acc, value_acc = accums
            safe_key = jnp.clip(key_id, 0, total_blocks - 1)
            allowed = block_mask(query_id, safe_key, target_counts)
            query_part, key_part, payload_portion = tile_grads(
                query_here[query_slot],
                grad_here[query_slot],
                key_here[key_slot],
                value_here[key_slot],
                allowed,
            )
            return (
                query_acc.at[query_slot].add(query_part),
                key_acc.at[key_slot].add(key_part),
                value_acc.at[key_slot].add(payload_portion),
            )

        return lax.cond(listed, work, lambda unchanged: unchanged, present_value)

    return lax.fori_loop(0, per_device * per_device, pair_step, grads)


def body(queries, keys, values, out_grad, key_blocks, target_counts):
    cycle_size = lax.axis_size("ctx")
    reach_hops = cycle_size // 4
    position = lax.axis_index("ctx")
    per_device = queries.shape[0] // BLK
    heads_here = queries.shape[1] // HEAD
    block_shape = (per_device, BLK, heads_here, HEAD)
    query_blocks = queries.reshape(block_shape)
    key_tiles = keys.reshape(block_shape)
    value_tiles = values.reshape(block_shape)
    grad_blocks = out_grad.reshape(block_shape)
    empty = jnp.zeros(block_shape, jnp.float32)

    def query_hop(hop_index, state):
        query_here, grad_here, query_acc, key_acc, value_acc = state
        source = position + hop_index
        query_acc, key_acc, value_acc = visit(
            source * per_device,
            position * per_device,
            source < cycle_size,
            query_here,
            grad_here,
            key_tiles,
            value_tiles,
            (query_acc, key_acc, value_acc),
            key_blocks,
            target_counts,
        )
        query_here, grad_here = from_behind((query_here, grad_here), "ctx", -1)
        query_acc = passed_along(query_acc, "ctx", -1)
        return (query_here, grad_here, query_acc, key_acc, value_acc)

    state = lax.fori_loop(
        0, reach_hops, query_hop, (query_blocks, grad_blocks, empty, empty, empty)
    )
    query_here, grad_here, query_acc, key_acc, value_acc = state
    source = position + reach_hops
    query_acc, key_acc, value_acc = visit(
        source * per_device,
        position * per_device,
        source < cycle_size,
        query_here,
        grad_here,
        key_tiles,
        value_tiles,
        (query_acc, key_acc, value_acc),
        key_blocks,
        target_counts,
    )
    query_acc = passed_along(query_acc.astype(jnp.bfloat16), "ctx", reach_hops).astype(
        query_acc.dtype
    )
    flat = queries.shape
    return (
        query_acc.reshape(flat).astype(jnp.bfloat16),
        key_acc.reshape(flat).astype(jnp.bfloat16),
        value_acc.reshape(flat).astype(jnp.bfloat16),
    )


def solution(mesh):
    in_specs = (P("ctx", "tp"), P("ctx", "tp"), P("ctx", "tp"), P("ctx", "tp"), P(), P())
    out_specs = (P("ctx", "tp"), P("ctx", "tp"), P("ctx", "tp"))
    length = mesh.shape["ctx"]
    mapped = functools.partial(near_body, length) if length // 4 == 2 else body
    return jax.shard_map(
        mapped, mesh=mesh, in_specs=in_specs, out_specs=out_specs, check_vma=False
    )
```

```python
import functools
import math

import jax
import jax.numpy as jnp
from jax import lax
from jax.experimental import pallas as pl
from jax.experimental.pallas import tpu as pltpu
from jax.sharding import PartitionSpec as P

HEAD = 128
BLK = 256
KPB = 16
MESH = pl.DeviceIdType.MESH
HEAD_FACTOR = 1.0 / math.sqrt(HEAD)
NORM_SCALE = 1.0 / math.sqrt(KPB * BLK)


def nt(a, b):
    return lax.dot_general(a, b, (((1,), (1,)), ((), ())), preferred_element_type=jnp.float32)


def tile(query, grad, key, value, key_columns, allowed=None):
    half = nt(key, query) * (0.5 * HEAD_FACTOR)
    one_tanh = 1.0 + jnp.tanh(half)
    weights = half * one_tanh
    score_grad = nt(value, grad) * (one_tanh + weights * (2.0 - one_tanh))
    if allowed is not None:
        weights = jnp.where(allowed, weights, 0.0)
        score_grad = jnp.where(allowed, score_grad, 0.0)
    weights = weights.astype(jnp.bfloat16)
    score_grad = score_grad.astype(jnp.bfloat16)
    value_part = jnp.dot(weights, grad, preferred_element_type=jnp.float32)
    key_part = jnp.dot(score_grad, query, preferred_element_type=jnp.float32)
    query_part = jnp.dot(key_columns, score_grad, preferred_element_type=jnp.float32)
    return query_part, key_part, value_part


def kernel(
    n, per, heads,
    blocks_ref, counts_ref, q_hbm, g_hbm, k_hbm, v_hbm,
    dq_hbm, dk_hbm, dv_hbm,
    dq_ref, dk_ref, dv_ref, qg_ref, k_ref, v_ref, kt_ref, r1, r2, dq1, dq2, rq1, rq2, dq0, dk_new, dv_new, dk_old, dv_old, mask,
    z_send, z_recv, y_send, y_recv, d1_send, d1_recv, d2_send, d2_recv, qg_own, kv_own, dq_out, dkv_out,
):
    p = lax.axis_index("ctx")
    total = n * per
    odd = lax.rem(p, 2) == 1
    even = lax.rem(p, 2) == 0
    has1, has2 = p + 1 < n, p + 2 < n
    back1, back2 = p >= 1, p >= 2
    next1, next2 = lax.rem(p + 1, n), lax.rem(p + 2, n)
    prev1, prev2 = lax.rem(p + n - 1, n), lax.rem(p + n - 2, n)
    partner = p + 1 - 2 * lax.rem(p, 2)
    first_core = lax.rem(lax.axis_index("tp"), 2) == 0
    second_core = lax.rem(lax.axis_index("tp"), 2) == 1
    chunks = heads * per
    lead = min(4, chunks)
    dq_scale = 0.5 * NORM_SCALE * HEAD_FACTOR

    def part(ref, c):
        rows = pl.ds(pl.multiple_of(lax.rem(c, per) * BLK, BLK), BLK)
        cols = pl.ds(pl.multiple_of(lax.div(c, per) * HEAD, HEAD), HEAD)
        return ref.at[rows, cols]

    def columns(ref, h):
        return ref.at[:, pl.ds(pl.multiple_of(h * HEAD, HEAD), HEAD)]

    def remote(src, dst, c, send, recv, to):
        return pltpu.make_async_remote_copy(
            src_ref=src.at[c], dst_ref=dst.at[c],
            send_sem=send.at[c], recv_sem=recv.at[c],
            device_id={"ctx": to}, device_id_type=MESH,
        )

    def qg_load(c):
        return [
            pltpu.make_async_copy(
                part(src, c), qg_ref.at[c, pl.ds(w * BLK, BLK)], qg_own.at[w, c]
            )
            for w, src in enumerate((q_hbm, g_hbm))
        ]

    def kv_load(h):
        return [
            pltpu.make_async_copy(columns(src, h), dst.at[h], kv_own.at[w, h])
            for w, (src, dst) in enumerate(((k_hbm, k_ref), (v_hbm, v_ref)))
        ]

    def dq_store(c):
        return pltpu.make_async_copy(dq_ref.at[c], part(dq_hbm, c), dq_out.at[c])

    def dkv_store(h):
        return [
            pltpu.make_async_copy(src.at[h], columns(dst, h), dkv_out.at[w, h])
            for w, (src, dst) in enumerate(((dk_ref, dk_hbm), (dv_ref, dv_hbm)))
        ]

    def z_copy(c):
        return remote(qg_ref, r2, c, z_send, z_recv, prev2)

    def y_copy(c, source):
        return remote(source, r1, c, y_send, y_recv, partner)

    def d1_copy(c):
        return remote(dq1, rq1, c, d1_send, d1_recv, next1)

    def d2_copy(c):
        return remote(dq2, rq2, c, d2_send, d2_recv, next2)

    def start_qg(c, carry):
        for load in qg_load(c):
            load.start()
        return carry

    def start_kv(h, carry):
        for load in kv_load(h):
            load.start()
        return carry

    def wait_kv(h, carry):
        for load in kv_load(h):
            load.wait()
        kt_ref[h] = k_ref[h].astype(jnp.float32).T.astype(jnp.bfloat16)
        return carry

    lax.fori_loop(0, chunks, start_qg, 0)
    lax.fori_loop(0, heads, start_kv, 0)

    barrier = pltpu.get_barrier_semaphore()
    for near, to in ((back1, prev1), (back2, prev2), (has1, next1), (has2, next2)):
        @pl.when(near)
        def _():
            pl.semaphore_signal(barrier, inc=1, device_id={"ctx": to}, device_id_type=MESH)
    pl.semaphore_wait(barrier, jnp.minimum(p, 2) + jnp.minimum(n - 1 - p, 2))

    def own_sends(c):
        @pl.when(back2 & first_core)
        def _():
            z_copy(c).start()

        @pl.when(odd)
        def _():
            y_copy(c, qg_ref).start()

        @pl.when(back2 & second_core)
        def _():
            z_copy(c).start()

    def loaded(c, carry):
        for load in qg_load(c):
            load.wait()
        return carry

    def first_sends(c, carry):
        loaded(c, carry)
        own_sends(c)
        return carry

    lax.fori_loop(0, lead, first_sends, 0)
    lax.fori_loop(lead, chunks, loaded, 0)

    row = lax.broadcasted_iota(jnp.int32, (BLK, HEAD), 0)
    for j in range(per):
        key_id = p * per + j
        kept = row < BLK - counts_ref[key_id]
        for d in range(3):
            for i in range(per):
                if (d == 0 and j >= i) or (d == 2 and j < i):
                    continue
                query_id = jnp.minimum((p + d) * per + i, total - 1)
                listed = jnp.int32(0)
                for slot in range(1, KPB):
                    listed = jnp.where(blocks_ref[slot, query_id] == key_id, 1, listed)
                mask[d * per + i, pl.ds(j * BLK, BLK), :] = jnp.where(
                    kept, listed.astype(jnp.float32), 0.0
                ).astype(jnp.bfloat16)

    key_row = lax.broadcasted_iota(jnp.int32, (BLK, BLK), 0)
    query_col = lax.broadcasted_iota(jnp.int32, (BLK, BLK), 1)

    dk_new[...] = jnp.zeros_like(dk_new)
    dv_new[...] = jnp.zeros_like(dv_new)
    lax.fori_loop(0, heads, wait_kv, 0)

    def source(d, h, i, qg, dk_sum, dv_sum):
        c = h * per + i
        query, grad = qg[c, pl.ds(0, BLK), :], qg[c, pl.ds(BLK, BLK), :]
        query_sum = None
        key_spans = {0: [(0, i), (i, 1)] if i else [(i, 1)], 1: [(0, per)], 2: [(i, per - i)]}
        for j, count in key_spans[d]:
            at = pl.ds(j * BLK, count * BLK)
            key, value, allowed = k_ref[h, at, :], v_ref[h, at, :], None
            if d == 0 and j == i:
                limit = BLK - counts_ref[p * per + i]
                allowed = (key_row <= query_col) & (
                    (key_row < limit) | (key_row == query_col)
                )
            else:
                read = mask[d * per + i, at, :]
                key, value = key * read, value * read
            query_part, key_part, value_part = tile(
                query, grad, key, value, kt_ref[h, :, at], allowed
            )
            query_sum = query_part if query_sum is None else query_sum + query_part
            dk_sum[at, :] += key_part
            dv_sum[at, :] += value_part
        return query_sum.T * dq_scale

    def one_round(h, carry):
        for i in range(per):
            @pl.when(h < heads)
            def _():
                c = h * per + i
                more = c + lead < chunks

                @pl.when(more & first_core)
                def _():
                    own_sends(c + lead)

                @pl.when(has2)
                def _():
                    z_copy(c).wait_recv()

                    @pl.when(even)
                    def _():
                        y_copy(c, r2).start()

                @pl.when(more & second_core)
                def _():
                    own_sends(c + lead)

                @pl.when(has2)
                def _():
                    dq2[c] = source(2, h, i, r2, dk_new, dv_new).astype(jnp.bfloat16)
                    d2_copy(c).start()

                dq0[c] = source(0, h, i, qg_ref, dk_new, dv_new)

            @pl.when((h > 0) & has1)
            def _():
                c = (h - 1) * per + i
                y_copy(c, qg_ref).wait_recv()
                part_sum = source(1, h - 1, i, r1, dk_old, dv_old)
                dq1[c] = part_sum.astype(jnp.bfloat16)
                d1_copy(c).start()

        @pl.when(h > 0)
        def _():
            dk_ref[h - 1] = (dk_old[...] * dq_scale).astype(jnp.bfloat16)
            dv_ref[h - 1] = (dv_old[...] * NORM_SCALE).astype(jnp.bfloat16)
            for store in dkv_store(h - 1):
                store.start()

        dk_old[...] = dk_new[...]
        dv_old[...] = dv_new[...]
        dk_new[...] = jnp.zeros_like(dk_new)
        dv_new[...] = jnp.zeros_like(dv_new)
        return carry

    lax.fori_loop(0, heads + 1, one_round, 0)

    def finish(c, carry):
        @pl.when(back2)
        def _():
            d2_copy(c).wait_recv()
            dq0[c] += rq2[c].astype(jnp.float32)
            z_copy(c).wait_send()

        @pl.when(back1)
        def _():
            d1_copy(c).wait_recv()
            dq0[c] += rq1[c].astype(jnp.float32)

        dq_ref[c] = dq0[c].astype(jnp.bfloat16)
        dq_store(c).start()

        @pl.when(odd | has2)
        def _():
            y_copy(c, qg_ref).wait_send()

        @pl.when(has1)
        def _():
            d1_copy(c).wait_send()

        @pl.when(has2)
        def _():
            d2_copy(c).wait_send()
        return carry

    lax.fori_loop(0, chunks, finish, 0)

    def stored(h, carry):
        for store in dkv_store(h):
            store.wait()
        for i in range(per):
            dq_store(h * per + i).wait()
        return carry

    lax.fori_loop(0, heads, stored, 0)


def hand_over(a_in, b_in, c_in, a_out, b_out, c_out, a, b, c, come, gone):
    half = a.shape[0] // 2
    steps = [
        (src.at[pl.ds(at, half)], held.at[pl.ds(at, half)], dst.at[pl.ds(at, half)])
        for src, held, dst in ((a_in, a, a_out), (b_in, b, b_out), (c_in, c, c_out))
        for at in (0, half)
    ]
    ins = [pltpu.make_async_copy(x, y, come.at[w]) for w, (x, y, _) in enumerate(steps)]
    outs = [pltpu.make_async_copy(y, z, gone.at[w]) for w, (_, y, z) in enumerate(steps)]
    for copy in ins:
        copy.start()
    for copy, later in zip(ins, outs):
        copy.wait()
        later.start()
    for copy in outs:
        copy.wait()


def near_body(n, queries, keys, values, out_grad, key_blocks, target_counts):
    rows, columns = queries.shape
    per, heads = rows // BLK, columns // HEAD
    chunks = heads * per
    narrow = pltpu.VMEM((rows, columns), jnp.bfloat16)
    by_chunk = pltpu.VMEM((chunks, BLK, HEAD), jnp.bfloat16)
    pairs = pltpu.VMEM((chunks, 2 * BLK, HEAD), jnp.bfloat16)
    by_head = pltpu.VMEM((heads, rows, HEAD), jnp.bfloat16)
    head_sum = pltpu.VMEM((rows, HEAD), jnp.float32)
    single = pltpu.SemaphoreType.DMA((chunks,))
    scalars = pl.BlockSpec(memory_space=pltpu.SMEM)
    result = jax.ShapeDtypeStruct((rows, columns), jnp.bfloat16)
    grads = pl.pallas_call(
        functools.partial(kernel, n, per, heads),
        out_shape=(result, result, result),
        in_specs=[scalars, scalars] + [pl.BlockSpec(memory_space=pl.ANY)] * 4,
        out_specs=(pl.BlockSpec(memory_space=pl.ANY),) * 3,
        scratch_shapes=[by_chunk, by_head, by_head, pairs, by_head, by_head]
        + [pltpu.VMEM((heads, HEAD, rows), jnp.bfloat16), pairs, pairs]
        + [by_chunk] * 4
        + [pltpu.VMEM((chunks, BLK, HEAD), jnp.float32)]
        + [head_sum] * 4
        + [pltpu.VMEM((3 * per, rows, HEAD), jnp.bfloat16)]
        + [single] * 8
        + [pltpu.SemaphoreType.DMA((2, chunks)), pltpu.SemaphoreType.DMA((2, heads))]
        + [single, pltpu.SemaphoreType.DMA((2, heads))],
        compiler_params=pltpu.CompilerParams(
            collective_id=0, has_side_effects=True, vmem_limit_bytes=56 * 1024 * 1024
        ),
    )(key_blocks.T, target_counts, queries, out_grad, keys, values)
    return pl.pallas_call(
        hand_over,
        out_shape=(result, result, result),
        in_specs=[pl.BlockSpec(memory_space=pl.ANY)] * 3,
        out_specs=(pl.BlockSpec(memory_space=pl.ANY),) * 3,
        scratch_shapes=[narrow] * 3 + [pltpu.SemaphoreType.DMA((6,))] * 2,
        compiler_params=pltpu.CompilerParams(vmem_limit_bytes=56 * 1024 * 1024),
    )(*grads)


def from_behind(array, axis, by):
    length = lax.axis_size(axis)
    pairs = [(i, i + by) for i in range(length) if 0 <= i + by < length]
    return lax.ppermute(array, axis, pairs)


def passed_along(array, axis, by):
    length = lax.axis_size(axis)
    return lax.ppermute(array, axis, [(i, (i + by) % length) for i in range(length)])


def block_mask(query_id, key_id, target_counts):
    row_index = jnp.arange(BLK, dtype=jnp.int32)[:, None]
    col_index = jnp.arange(BLK, dtype=jnp.int32)[None, :]
    own_targets = target_counts[query_id]
    key_targets = target_counts[key_id]
    diagonal = (col_index <= row_index) & (
        (col_index < BLK - own_targets) | (col_index == row_index)
    )
    earlier = jnp.broadcast_to(col_index < BLK - key_targets, diagonal.shape)
    return jnp.where(query_id == key_id, diagonal, earlier).astype(jnp.float32)


def tile_grads(query_tile, grad_tile, key_tile, value_tile, allowed):
    head_factor = 1.0 / math.sqrt(HEAD)
    norm_scale = 1.0 / math.sqrt(KPB * BLK)
    scores = (
        jnp.einsum("ihd,jhd->hij", query_tile, key_tile, preferred_element_type=jnp.float32)
        * head_factor
    )
    sigmoid_part = jax.nn.sigmoid(scores)
    gated = allowed[None] * norm_scale
    weights = (scores * sigmoid_part * gated).astype(jnp.bfloat16)
    weight_grad = jnp.einsum(
        "ihd,jhd->hij", grad_tile, value_tile, preferred_element_type=jnp.float32
    )
    score_grad = (
        weight_grad * gated * sigmoid_part * (1.0 + scores * (1.0 - sigmoid_part))
    ).astype(jnp.bfloat16)
    query_part = (
        jnp.einsum("hij,jhd->ihd", score_grad, key_tile, preferred_element_type=jnp.float32)
        * head_factor
    )
    key_part = (
        jnp.einsum("hij,ihd->jhd", score_grad, query_tile, preferred_element_type=jnp.float32)
        * head_factor
    )
    payload_portion = jnp.einsum(
        "hij,ihd->jhd", weights, grad_tile, preferred_element_type=jnp.float32
    )
    return (query_part, key_part, payload_portion)


def visit(
    query_base,
    key_base,
    active,
    query_here,
    grad_here,
    key_here,
    value_here,
    grads,
    key_blocks,
    target_counts,
):
    per_device = query_here.shape[0]
    total_blocks = key_blocks.shape[0]

    def pair_step(pair_index, present_value):
        query_slot = pair_index // per_device
        key_slot = pair_index % per_device
        query_id = jnp.clip(query_base + query_slot, 0, total_blocks - 1)
        key_id = key_base + key_slot
        listed = active & jnp.any(key_blocks[query_id] == key_id)

        def work(accums):
            query_acc, key_acc, value_acc = accums
            safe_key = jnp.clip(key_id, 0, total_blocks - 1)
            allowed = block_mask(query_id, safe_key, target_counts)
            query_part, key_part, payload_portion = tile_grads(
                query_here[query_slot],
                grad_here[query_slot],
                key_here[key_slot],
                value_here[key_slot],
                allowed,
            )
            return (
                query_acc.at[query_slot].add(query_part),
                key_acc.at[key_slot].add(key_part),
                value_acc.at[key_slot].add(payload_portion),
            )

        return lax.cond(listed, work, lambda unchanged: unchanged, present_value)

    return lax.fori_loop(0, per_device * per_device, pair_step, grads)


def body(queries, keys, values, out_grad, key_blocks, target_counts):
    cycle_size = lax.axis_size("ctx")
    reach_hops = cycle_size // 4
    position = lax.axis_index("ctx")
    per_device = queries.shape[0] // BLK
    heads_here = queries.shape[1] // HEAD
    block_shape = (per_device, BLK, heads_here, HEAD)
    query_blocks = queries.reshape(block_shape)
    key_tiles = keys.reshape(block_shape)
    value_tiles = values.reshape(block_shape)
    grad_blocks = out_grad.reshape(block_shape)
    empty = jnp.zeros(block_shape, jnp.float32)

    def query_hop(hop_index, state):
        query_here, grad_here, query_acc, key_acc, value_acc = state
        source = position + hop_index
        query_acc, key_acc, value_acc = visit(
            source * per_device,
            position * per_device,
            source < cycle_size,
            query_here,
            grad_here,
            key_tiles,
            value_tiles,
            (query_acc, key_acc, value_acc),
            key_blocks,
            target_counts,
        )
        query_here, grad_here = from_behind((query_here, grad_here), "ctx", -1)
        query_acc = passed_along(query_acc, "ctx", -1)
        return (query_here, grad_here, query_acc, key_acc, value_acc)

    state = lax.fori_loop(
        0, reach_hops, query_hop, (query_blocks, grad_blocks, empty, empty, empty)
    )
    query_here, grad_here, query_acc, key_acc, value_acc = state
    source = position + reach_hops
    query_acc, key_acc, value_acc = visit(
        source * per_device,
        position * per_device,
        source < cycle_size,
        query_here,
        grad_here,
        key_tiles,
        value_tiles,
        (query_acc, key_acc, value_acc),
        key_blocks,
        target_counts,
    )
    query_acc = passed_along(query_acc.astype(jnp.bfloat16), "ctx", reach_hops).astype(
        query_acc.dtype
    )
    flat = queries.shape
    return (
        query_acc.reshape(flat).astype(jnp.bfloat16),
        key_acc.reshape(flat).astype(jnp.bfloat16),
        value_acc.reshape(flat).astype(jnp.bfloat16),
    )


def solution(mesh):
    in_specs = (P("ctx", "tp"), P("ctx", "tp"), P("ctx", "tp"), P("ctx", "tp"), P(), P())
    out_specs = (P("ctx", "tp"), P("ctx", "tp"), P("ctx", "tp"))
    length = mesh.shape["ctx"]
    mapped = functools.partial(near_body, length) if length // 4 == 2 else body
    return jax.shard_map(
        mapped, mesh=mesh, in_specs=in_specs, out_specs=out_specs, check_vma=False
    )
```
